32 devices in a mesh: groups: 2 (over x), tile: 8 (over z, y), tm: 2 (over core).
Axes of the slice: x: 2, y: 2, z: 4, core: 2. Of those that a mesh axis runs over, the one named last changes fastest.
Arguments:
- pixels: bfloat16 [64, 3, 64, 1280], P(('groups', 'tile', 'tm')), parts along dimension 0, may hold values from -1 to 1
- owner: int32 [32], P('groups'), parts along dimension 0, may hold values from 0 to 15, as said below
- patch_weight: bfloat16 [768, 1024], replicated, may hold values from -0.21875 to 0.21875
- norm_gain: float32 [1024], replicated, may hold values from 0.25 to 1.75
- qkv_weight: bfloat16 [1024, 3072], replicated, may hold values from -0.1875 to 0.1875
- out_weight: bfloat16 [1024, 1024], replicated, may hold values from -0.1875 to 0.1875
- post_gain: float32 [1024], replicated, may hold values from 0.25 to 1.75
- text_embed: float32 [2048], P('groups'), parts along dimension 0, may hold values from -6 to 6
- conv_out_weight: bfloat16 [3, 3, 128, 3], replicated, may hold values from -1.25 to 1.25
- conv_weight: bfloat16 [3, 3, 128, 128], replicated, may hold values from -0.1875 to 0.1875
- activations: bfloat16 [32, 64, 1280, 128], P(('groups', 'tm'), None, 'tile'), parts along dimension 0, may hold values from -8 to 8
Outputs:
- input_grad: bfloat16 [32, 64, 1280, 128], P(('groups', 'tm'), None, 'tile'), parts along dimension 0
The draws below stay inside these ranges and needn't reach their ends.
There are 2 independent parts, one for each index of `groups`. The reference program is written for one: setup_inputs(seed, part) draws one part's arguments, and reference() takes and returns one part's arrays. A program takes and returns all parts, laid end to end along the dimension named above; an argument that names none is the same for every part. Nothing has to cross between parts.
Inputs may be any that keep to these rules, and one draw needn't show every extreme that they name: Each owner holds at most 2 frames, and one owner holds exactly 2.
All inputs are finite; a program needn't handle non-finite values.
Results may differ from the reference program's by a relative error of at most 0.018.
Values may be sent and summed in bfloat16 or wider, within the bound.
No kernel may reach another device: no remote copies, remote signals or barrier semaphores. Data moves between devices by JAX's collectives and lax.ppermute only.
A program may use at most 192 MiB of HBM per device.

```python
import jax
import jax.numpy as jnp
from jax import lax

D = 1024
HEADS = 16
HEAD_DIM = 64
PATCH = 16
CH = 128
COLS = 1280
ROWS = 64
MOST = 2
PATCH_DIM = 768
F = 16
OWNERS = 16


def draw_owner(key, part):
    key = jax.random.fold_in(key, 11)
    key_busy, key_order, key_rest = jax.random.split(key, 3)
    busiest = jax.random.randint(key_busy, (), 0, OWNERS, dtype=jnp.int32)
    frame_order = jax.random.permutation(key_order, F)
    others = (jax.random.permutation(key_rest, (OWNERS - 1) * MOST)[:F - MOST] // MOST).astype(jnp.int32)
    others = others + (others >= busiest).astype(jnp.int32)
    by_order = jnp.concatenate([jnp.full((MOST,), busiest, jnp.int32), others])
    return jnp.zeros((F,), jnp.int32).at[frame_order].set(by_order)


def shard_levels(stream_key, extent, shards, low, top_value):
    factor_of, own = 1.0, jax.random.fold_in(stream_key, 6)
    for dim, parts in shards:
        heights = jnp.exp(jax.random.uniform(jax.random.fold_in(own, dim), (parts,), jnp.float32, low / len(shards), top_value / len(shards)))
        factor_of = factor_of * jnp.repeat(heights, extent[dim] // parts).reshape([-1 if axis == dim else 1 for axis in range(len(extent))])
    return factor_of


def gaussian(own_key, dims, deviation, reach, shards=(), held_as=jnp.bfloat16):
    array = jax.random.normal(own_key, dims, jnp.float32) * deviation
    if len(shards) > 0:
        array = shard_levels(own_key, dims, shards, -0.22, 0.18) * array
    return jnp.clip(array, min=-reach, max=reach).astype(held_as)


def setup_inputs(seed: int = 0, part: int = 0) -> dict:
    streams_of = jax.random.split(jax.random.key(seed), 12)
    part_keys = jax.random.split(jax.random.fold_in(streams_of[11], part), 12)
    return {
        "pixels": jnp.clip(jax.random.uniform(part_keys[0], (OWNERS * MOST, 3, ROWS, COLS), jnp.float32, -1.0, 1.0) * shard_levels(part_keys[0], (OWNERS * MOST, 3, ROWS, COLS), ((0, 16),), -0.4, 0.0), -1.0, 1.0).astype(jnp.bfloat16),
        "owner": draw_owner(jax.random.fold_in(jax.random.fold_in(streams_of[11], part), 71), part),
        "patch_weight": gaussian(streams_of[2], (PATCH_DIM, D), PATCH_DIM ** -0.5, 0.21875),
        "norm_gain": jnp.clip(1.0 + 0.15 * jax.random.normal(streams_of[3], (D,), jnp.float32), 0.25, 1.75),
        "qkv_weight": gaussian(streams_of[4], (D, 3 * D), D ** -0.5, 0.1875),
        "out_weight": gaussian(streams_of[5], (D, D), D ** -0.5, 0.1875),
        "post_gain": jnp.clip(1.0 + 0.15 * jax.random.normal(streams_of[6], (D,), jnp.float32), 0.25, 1.75),
        "text_embed": gaussian(part_keys[7], (D,), 1.0, 6.0, (), jnp.float32),
        "conv_out_weight": gaussian(streams_of[8], (3, 3, CH, 3), 27 ** -0.5, 1.25),
        "conv_weight": gaussian(streams_of[9], (3, 3, CH, CH), (9 * CH) ** -0.5, 0.1875),
        "activations": gaussian(part_keys[10], (F, ROWS, COLS, CH), 1.5, 8.0, ((0, 2), (2, 8))),
    }


EPS = 1e-06
LOGIT_SCALE = 100.0
LOSS_SCALE = 64.0

def plain_norm(values):
    centred = values - lax.optimization_barrier(jnp.mean(values, axis=-1, keepdims=True))
    spread = lax.optimization_barrier(jnp.mean(centred * centred, axis=-1, keepdims=True))
    return centred * lax.rsqrt(spread + EPS)

def frame_rank(owner):
    frame_ids = jnp.arange(owner.shape[0], dtype=jnp.int32)
    same_owner = owner[:, None] == owner[None, :]
    earlier = frame_ids[None, :] < frame_ids[:, None]
    return lax.optimization_barrier(jnp.sum((same_owner & earlier).astype(jnp.int32), axis=1)).astype(jnp.int32)

def unit_vector(text_embed):
    return text_embed * lax.rsqrt(jnp.sum(text_embed * text_embed) + EPS)

def to_patches(one_frame):
    patch_rows = one_frame.shape[1] // PATCH
    patch_cols = one_frame.shape[2] // PATCH
    blocks = one_frame.reshape(3, patch_rows, PATCH, patch_cols, PATCH)
    return blocks.transpose(1, 3, 0, 2, 4).reshape(patch_rows * patch_cols, 3 * PATCH * PATCH)

def from_patches(patches, height, width):
    patch_rows = height // PATCH
    patch_cols = width // PATCH
    blocks = patches.reshape(patch_rows, patch_cols, 3, PATCH, PATCH)
    return blocks.transpose(2, 0, 3, 1, 4).reshape(3, height, width)

def scaled_loss(embedded, norm_gain, qkv_weight, out_weight, post_gain, text_unit):
    tokens_count = embedded.shape[0]
    normed = (plain_norm(embedded) * norm_gain).astype(jnp.bfloat16)
    projected = jnp.dot(normed, qkv_weight, preferred_element_type=jnp.float32)
    projected = projected.reshape(tokens_count, 3, HEADS, HEAD_DIM)
    query_rows = plain_norm(projected[:, 0]).astype(jnp.bfloat16)
    key_rows = plain_norm(projected[:, 1]).astype(jnp.bfloat16)
    value_rows = projected[:, 2].astype(jnp.bfloat16)
    scores = jnp.einsum('qhd,khd->hqk', query_rows.astype(jnp.float32), key_rows.astype(jnp.float32))
    scores = scores * (1.0 / HEAD_DIM ** 0.5)
    exp_scores = jnp.exp(scores)
    attn_probs = (exp_scores / lax.optimization_barrier(jnp.sum(exp_scores, axis=-1, keepdims=True))).astype(jnp.bfloat16)
    context = jnp.einsum('hqk,khd->qhd', attn_probs.astype(jnp.float32), value_rows.astype(jnp.float32))
    context = context.astype(jnp.bfloat16).reshape(tokens_count, HEADS * HEAD_DIM)
    attended = embedded + jnp.dot(context, out_weight, preferred_element_type=jnp.float32)
    pooled = lax.optimization_barrier(jnp.mean(attended, axis=0))
    post_norm = plain_norm(pooled) * post_gain
    cosine = jnp.sum(post_norm * text_unit) * lax.rsqrt(jnp.sum(post_norm * post_norm) + EPS)
    return LOSS_SCALE * LOGIT_SCALE * cosine

def frame_gradient(one_frame, patch_weight, norm_gain, qkv_weight, out_weight, post_gain, text_unit):
    patches = to_patches(one_frame)
    embedded = jnp.dot(patches, patch_weight, preferred_element_type=jnp.float32)
    tangent = jax.grad(scaled_loss)(embedded, norm_gain, qkv_weight, out_weight, post_gain, text_unit)
    back_patches = jnp.dot(tangent.astype(jnp.bfloat16), patch_weight.T, preferred_element_type=jnp.float32)
    return from_patches(back_patches, one_frame.shape[1], one_frame.shape[2]).astype(jnp.bfloat16)

def decoder_frame(pixel_grad, pre_act, conv_out_weight, conv_weight):
    height = pixel_grad.shape[1]
    width = pixel_grad.shape[2]
    rimmed = jnp.pad(pixel_grad, ((0, 0), (1, 1), (1, 1)))
    back_sum = jnp.zeros((height, width, conv_out_weight.shape[2]), jnp.float32)
    for row_tap in range(3):
        for col_tap in range(3):
            shifted = rimmed[:, 2 - row_tap:2 - row_tap + height, 2 - col_tap:2 - col_tap + width]
            back_sum = back_sum + jnp.einsum('kyx,ck->yxc', shifted.astype(jnp.float32), conv_out_weight[row_tap, col_tap].astype(jnp.float32))
    pre_value = pre_act.astype(jnp.float32)
    sig_gate = jax.nn.sigmoid(pre_value)
    act_grad = (back_sum * sig_gate * (1.0 + pre_value * (1.0 - sig_gate))).astype(jnp.bfloat16)
    rimmed_act = jnp.pad(act_grad, ((1, 1), (1, 1), (0, 0)))
    summed = act_grad.astype(jnp.float32)
    for row_tap in range(3):
        for col_tap in range(3):
            shifted = rimmed_act[2 - row_tap:2 - row_tap + height, 2 - col_tap:2 - col_tap + width, :]
            summed = summed + jnp.einsum('yxk,ck->yxc', shifted.astype(jnp.float32), conv_weight[row_tap, col_tap].astype(jnp.float32))
    return summed.astype(jnp.bfloat16)

def reference(pixels, owner, patch_weight, norm_gain, qkv_weight, out_weight, post_gain, text_embed, conv_out_weight, conv_weight, activations):
    ranks_all = frame_rank(owner)
    slot_index = (owner * MOST + ranks_all).astype(jnp.int32)
    text_unit = unit_vector(text_embed)

    def score_one(position):
        one_frame = jnp.take(pixels, position, axis=0)
        return frame_gradient(one_frame, patch_weight, norm_gain, qkv_weight, out_weight, post_gain, text_unit)
    grad_frames = lax.map(score_one, slot_index)

    def decode_one(pair):
        return decoder_frame(pair[0], pair[1], conv_out_weight, conv_weight)
    return lax.map(decode_one, (grad_frames, activations))
```

```python
import functools

import jax
import jax.numpy as jnp
from jax import lax
from jax.experimental import pallas as pl
from jax.experimental.pallas import tpu as pltpu
from jax.sharding import PartitionSpec as P

HEADS = 16
HEAD_DIM = 64
PATCH = 16
EPS = 1e-06
LOGIT_SCALE = 100.0
LOSS_SCALE = 64.0

LANES = 128
SUB = 16


def silu_slope(pre_value):
    half = jnp.tanh(0.5 * pre_value)
    return 0.5 + 0.5 * half + (0.25 * pre_value) * (1.0 - half * half)


def decoder_kernel(
    height,
    width,
    block_rows,
    pick_ref,
    own_ref,
    near_ref,
    far_ref,
    left_ref,
    right_ref,
    act_ref,
    w_edge_ref,
    w_one_ref,
    w_two_ref,
    out_ref,
    taps_ref,
    row_ref,
    edge_ref,
    grads_ref,
):
    frame = pl.program_id(0)
    rem = max(width + 4 - LANES, 0)
    chunks = -(-width // LANES)

    @pl.when(frame == 0)
    def _():
        taps_ref[...] = jnp.zeros_like(taps_ref)
        for s in range(3):
            zero_row = jnp.zeros(grads_ref.shape[2:], grads_ref.dtype)
            grads_ref[s, 0] = zero_row
            grads_ref[s, height + 1] = zero_row

    is_near = own_ref[frame] != 0
    message = jnp.where(is_near, near_ref[0].astype(jnp.float32), far_ref[0].astype(jnp.float32))
    mains = [message[k * height : (k + 1) * height] for k in range(3)]
    if rem > 0:
        tail = message[3 * height : 4 * height]
    for k in range(3):
        if rem > 0:
            line = jnp.concatenate([mains[k], tail[:, k * rem : (k + 1) * rem]], axis=1)
        else:
            line = mains[k]
        for s in range(3):
            for c in range(chunks):
                start = 3 - s + c * LANES
                stop = min(start + LANES, width + 4)
                part = line[:, start:stop]
                if stop - start < LANES:
                    blank = jnp.zeros((height, LANES - (stop - start)), jnp.float32)
                    part = jnp.concatenate([part, blank], axis=1)
                taps_ref[c, pl.ds(SUB + 3 * s + k, height, stride=SUB), :] = part
    pieces = mains + ([tail] if rem > 0 else [])
    wide = jnp.concatenate(pieces, axis=1).astype(jnp.bfloat16)
    per_tap = jnp.dot(wide, w_edge_ref[...], preferred_element_type=jnp.float32)
    zeros = jnp.zeros((1, 2 * LANES), jnp.float32)
    first, middle, last = (per_tap[:, i * 2 * LANES : (i + 1) * 2 * LANES] for i in range(3))
    edge = (
        jnp.concatenate([first[1:], zeros], axis=0)
        + middle
        + jnp.concatenate([zeros, last[: height - 1]], axis=0)
    )
    edge_ref[:, :LANES] = edge[:, :LANES] * silu_slope(left_ref[0].astype(jnp.float32))
    edge_ref[:, LANES:] = edge[:, LANES:] * silu_slope(right_ref[0].astype(jnp.float32))

    pairs = block_rows // 2

    def produce(block):
        base = block * block_rows
        lhs = jnp.concatenate(
            [
                taps_ref[c, (base + 2 * p) * SUB : (base + 2 * p + 4) * SUB, :]
                .T[: min(LANES, width - c * LANES)]
                .astype(jnp.bfloat16)
                for p in range(pairs)
                for c in range(chunks)
            ],
            axis=0,
        )
        back = jnp.dot(lhs, w_one_ref[...], preferred_element_type=jnp.float32)
        for i in range(block_rows):
            y = base + i
            p, h = i // 2, i % 2
            part = back[p * width : (p + 1) * width, h * LANES : (h + 1) * LANES]
            value = part * silu_slope(act_ref[0, y].astype(jnp.float32))
            slot = i % 4
            row_ref[slot, 8 : 8 + width, :] = value
            row_ref[slot, 7:8, :] = edge_ref[y : y + 1, :LANES]
            row_ref[slot, 8 + width : 9 + width, :] = edge_ref[y : y + 1, LANES:]
            grads_ref[0, y + 1] = row_ref[slot, 9 : 9 + width, :].astype(jnp.bfloat16)
            grads_ref[1, y + 1] = value.astype(jnp.bfloat16)
            grads_ref[2, y + 1] = row_ref[slot, 7 : 7 + width, :].astype(jnp.bfloat16)

    def consume(block):
        base = block * block_rows
        total = None
        slabs = []
        for j in range(4):
            for s in range(3):
                slabs.append(
                    jnp.concatenate([grads_ref[s, base + 2 * p + j] for p in range(pairs)], axis=0)
                )
        lhs = jnp.concatenate(slabs, axis=1)
        total = jnp.dot(lhs, w_two_ref[...], preferred_element_type=jnp.float32)
        for i in range(block_rows):
            p, h = i // 2, i % 2
            part = total[p * width : (p + 1) * width, h * LANES : (h + 1) * LANES]
            centre = grads_ref[1, base + i + 1].astype(jnp.float32)
            out_ref[0, base + i] = (part + centre).astype(out_ref.dtype)

    blocks = height // block_rows
    produce(0)
    for block in range(blocks):
        if block + 1 < blocks:
            produce(block + 1)
        consume(block)


def decoder_weights(conv_out_weight, conv_weight, height, width):
    rem = max(width + 4 - LANES, 0)
    taps_out = conv_out_weight.transpose(0, 1, 3, 2)
    channels = conv_weight.shape[2]
    small = jnp.pad(
        taps_out.reshape(3, 9, channels), ((0, 0), (0, SUB - 9), (0, 0))
    )
    none = jnp.zeros_like(small[0])
    w_one = jnp.concatenate(
        [
            jnp.stack([small[h - j + 2] if 0 <= h - j + 2 < 3 else none for j in range(4)])
            for h in range(2)
        ],
        axis=2,
    ).reshape(4 * SUB, 2 * channels)
    big = conv_weight.transpose(0, 1, 3, 2)
    none = jnp.zeros_like(big[0])
    w_two = jnp.concatenate(
        [
            jnp.stack([big[h - j + 2] if 0 <= h - j + 2 < 3 else none for j in range(4)])
            for h in range(2)
        ],
        axis=3,
    ).reshape(4 * 3 * channels, 2 * channels)
    flipped = taps_out[:, ::-1].transpose(0, 2, 1, 3)
    groups = 4 if rem > 0 else 3
    sides = []
    for r in range(3):
        left = jnp.zeros((groups * LANES, channels), conv_out_weight.dtype)
        right = jnp.zeros((groups * LANES, channels), conv_out_weight.dtype)
        for k in range(3):
            left = left.at[k * LANES : k * LANES + 3].set(flipped[r, k])
            for i in range(3):
                lane = width + 1 + i
                if lane < LANES:
                    place = k * LANES + lane
                else:
                    place = 3 * LANES + k * rem + lane - LANES
                right = right.at[place].set(flipped[r, k, i])
        sides.extend([left, right])
    w_edge = jnp.concatenate(sides, axis=1)
    return w_edge, w_one, w_two


def decode(pick, own, near, far, left, right, activations, conv_out_weight, conv_weight, block_rows):
    frames, height, width, channels = activations.shape
    rows = near.shape[1]
    w_edge, w_one, w_two = decoder_weights(conv_out_weight, conv_weight, height, width)
    whole = lambda shape: pl.BlockSpec(shape, lambda f, *_: (0,) * len(shape))
    padded = -(-(width + 9) // 8) * 8 + 8
    return pl.pallas_call(
        functools.partial(decoder_kernel, height, width, block_rows),
        out_shape=jax.ShapeDtypeStruct(activations.shape, jnp.bfloat16),
        grid_spec=pltpu.PrefetchScalarGridSpec(
            num_scalar_prefetch=2,
            grid=(frames,),
            in_specs=[
                pl.BlockSpec((1, rows, LANES), lambda f, pick, own: (pick[f], 0, 0)),
                pl.BlockSpec((1, rows, LANES), lambda f, pick, own: (f, 0, 0)),
                pl.BlockSpec((1, height, channels), lambda f, *_: (f, 0, 0)),
                pl.BlockSpec((1, height, channels), lambda f, *_: (f, 0, 0)),
                pl.BlockSpec((1, height, width, channels), lambda f, *_: (f, 0, 0, 0)),
                whole(w_edge.shape),
                whole(w_one.shape),
                whole(w_two.shape),
            ],
            out_specs=pl.BlockSpec((1, height, width, channels), lambda f, *_: (f, 0, 0, 0)),
            scratch_shapes=[
                pltpu.VMEM((-(-width // LANES), (height + 2) * SUB, LANES), jnp.float32),
                pltpu.VMEM((4, padded, channels), jnp.float32),
                pltpu.VMEM((height, 2 * channels), jnp.float32),
                pltpu.VMEM((3, height + 2, width, channels), jnp.bfloat16),
            ],
        ),
        compiler_params=pltpu.CompilerParams(vmem_limit_bytes=56 * 1024 * 1024),
        cost_estimate=pl.CostEstimate(
            flops=2 * frames * height * width * channels * (12 * channels + 64),
            bytes_accessed=4 * frames * height * width * channels,
            transcendentals=frames * height * width * channels,
        ),
    )(pick, own, near, far, left, right, activations, w_edge, w_one, w_two)


def plain_norm(values):
    centred = values - jnp.mean(values, axis=-1, keepdims=True)
    spread = jnp.mean(centred * centred, axis=-1, keepdims=True)
    return centred * lax.rsqrt(spread + EPS)


def frame_rank(owner):
    frame_ids = jnp.arange(owner.shape[0], dtype=jnp.int32)
    same_owner = owner[:, None] == owner[None, :]
    earlier = frame_ids[None, :] < frame_ids[:, None]
    return jnp.sum((same_owner & earlier).astype(jnp.int32), axis=1)


def unit_vector(text_embed):
    return text_embed * lax.rsqrt(jnp.sum(text_embed * text_embed) + EPS)


def to_patches(one_frame):
    patch_rows = one_frame.shape[1] // PATCH
    patch_cols = one_frame.shape[2] // PATCH
    blocks = one_frame.reshape(3, patch_rows, PATCH, patch_cols, PATCH)
    return blocks.transpose(1, 3, 0, 2, 4).reshape(patch_rows * patch_cols, 3 * PATCH * PATCH)


def from_patches(patches, height, width):
    patch_rows = height // PATCH
    patch_cols = width // PATCH
    blocks = patches.reshape(patch_rows, patch_cols, 3, PATCH, PATCH)
    return blocks.transpose(2, 0, 3, 1, 4).reshape(3, height, width)


def scaled_loss(embedded, norm_gain, qkv_weight, out_weight, post_gain, text_unit):
    tokens_count = embedded.shape[0]
    normed = (plain_norm(embedded) * norm_gain).astype(jnp.bfloat16)
    projected = jnp.dot(normed, qkv_weight, preferred_element_type=jnp.float32)
    projected = projected.reshape(tokens_count, 3, HEADS, HEAD_DIM)
    query_rows = plain_norm(projected[:, 0]).astype(jnp.bfloat16)
    key_rows = plain_norm(projected[:, 1]).astype(jnp.bfloat16)
    value_rows = projected[:, 2].astype(jnp.bfloat16)
    scores = jnp.einsum(
        "qhd,khd->hqk", query_rows.astype(jnp.float32), key_rows.astype(jnp.float32)
    )
    scores = scores * (1.0 / HEAD_DIM**0.5)
    exp_scores = jnp.exp(scores)
    attn_probs = (exp_scores / jnp.sum(exp_scores, axis=-1, keepdims=True)).astype(jnp.bfloat16)
    context = jnp.einsum(
        "hqk,khd->qhd", attn_probs.astype(jnp.float32), value_rows.astype(jnp.float32)
    )
    context = context.astype(jnp.bfloat16).reshape(tokens_count, HEADS * HEAD_DIM)
    attended = embedded + jnp.dot(context, out_weight, preferred_element_type=jnp.float32)
    pooled = jnp.mean(attended, axis=0)
    post_norm = plain_norm(pooled) * post_gain
    cosine = jnp.sum(post_norm * text_unit) * lax.rsqrt(jnp.sum(post_norm * post_norm) + EPS)
    return LOSS_SCALE * LOGIT_SCALE * cosine


def frame_gradient(
    one_frame, patch_weight, norm_gain, qkv_weight, out_weight, post_gain, text_unit
):
    patches = to_patches(one_frame)
    embedded = jnp.dot(patches, patch_weight, preferred_element_type=jnp.float32)
    tangent = jax.grad(scaled_loss)(
        embedded, norm_gain, qkv_weight, out_weight, post_gain, text_unit
    )
    back_patches = jnp.dot(
        tangent.astype(jnp.bfloat16), patch_weight.T, preferred_element_type=jnp.float32
    )
    return from_patches(back_patches, one_frame.shape[1], one_frame.shape[2]).astype(jnp.bfloat16)


def pack_strips(grad_frames, tile_count, width):
    slots, colours, height, columns = grad_frames.shape
    padded = jnp.pad(grad_frames, ((0, 0), (0, 0), (0, 0), (2, 2)))
    strips = jnp.stack(
        [padded[..., t * width : t * width + width + 4] for t in range(tile_count)]
    )
    main = strips[..., :LANES]
    main = jnp.pad(main, ((0, 0),) * 4 + ((0, LANES - main.shape[-1]),))
    main = main.reshape(tile_count, slots, colours * height, LANES)
    if width + 4 <= LANES:
        return main
    tail = strips[..., LANES:].transpose(0, 1, 3, 2, 4).reshape(tile_count, slots, height, -1)
    tail = jnp.pad(tail, ((0, 0),) * 3 + ((0, LANES - tail.shape[-1]),))
    return jnp.concatenate([main, tail], axis=2)


def local(
    pixels,
    owner,
    patch_weight,
    norm_gain,
    qkv_weight,
    out_weight,
    post_gain,
    text_embed,
    conv_out_weight,
    conv_weight,
    activations,
):
    tile_count = lax.axis_size("tile")
    core_count = lax.axis_size("tm")
    core = lax.axis_index("tm")
    tile = lax.axis_index("tile")
    frames, height, width, channels = activations.shape
    slots = pixels.shape[0]
    ranks_all = frame_rank(owner)
    text_unit = unit_vector(text_embed)

    up = [(i, i + 1) for i in range(tile_count - 1)]
    down = [(j, i) for i, j in up]
    outside = jnp.asarray(-30000.0, activations.dtype)
    left = lax.ppermute(activations[:, :, width - 1], "tile", up)
    right = lax.ppermute(activations[:, :, 0], "tile", down)
    left = jnp.where(tile == 0, outside, left)
    right = jnp.where(tile == tile_count - 1, outside, right)

    def score_one(one_frame):
        return frame_gradient(
            one_frame, patch_weight, norm_gain, qkv_weight, out_weight, post_gain, text_unit
        )

    grad_frames = lax.map(score_one, pixels)
    outgoing = pack_strips(grad_frames, tile_count, width)
    rows = outgoing.shape[2]
    near = lax.all_to_all(outgoing, "tile", split_axis=0, concat_axis=0, tiled=True)
    near = near.reshape(tile_count * slots, rows, LANES)
    pick_all = (owner // core_count) * slots + ranks_all
    own_all = owner % core_count
    by_core = lambda values, index: lax.dynamic_slice_in_dim(values, index * frames, frames)
    other = 1 - core
    far = lax.ppermute(jnp.take(near, by_core(pick_all, other), axis=0), "tm", [(0, 1), (1, 0)])
    return decode(
        by_core(pick_all, core),
        (by_core(own_all, core) == core).astype(jnp.int32),
        near,
        far,
        left,
        right,
        activations,
        conv_out_weight,
        conv_weight,
        4,
    )


def solution(mesh):
    placed = (
        P(("groups", "tile", "tm"), None, None, None),
        P("groups"),
        P(),
        P(),
        P(),
        P(),
        P(),
        P("groups"),
        P(),
        P(),
        P(("groups", "tm"), None, "tile", None),
    )
    return jax.shard_map(
        local,
        mesh=mesh,
        in_specs=placed,
        out_specs=P(("groups", "tm"), None, "tile", None),
        check_vma=False,
    )
```

```python
import functools

import jax
import jax.numpy as jnp
from jax import lax
from jax.experimental import pallas as pl
from jax.experimental.pallas import tpu as pltpu
from jax.sharding import PartitionSpec as P

HEADS = 16
HEAD_DIM = 64
PATCH = 16
EPS = 1e-06
LOGIT_SCALE = 100.0
LOSS_SCALE = 64.0

LANES = 128
SUB = 16
NARROW = jnp.bfloat16
WIDE = jnp.float32


def silu_slope(pre_value):
    half = jnp.tanh(0.5 * pre_value)
    return 0.5 + 0.5 * half + (0.25 * pre_value) * (1.0 - half * half)


def decoder_kernel(
    height,
    width,
    block_rows,
    pick_ref,
    own_ref,
    near_ref,
    far_ref,
    left_ref,
    right_ref,
    act_ref,
    w_edge_ref,
    w_one_ref,
    w_two_ref,
    out_ref,
    taps_ref,
    row_ref,
    edge_ref,
    grads_ref,
):
    frame = pl.program_id(0)
    rem = max(width + 4 - LANES, 0)
    chunks = -(-width // LANES)

    @pl.when(frame == 0)
    def _():
        taps_ref[...] = jnp.zeros_like(taps_ref)
        for s in range(3):
            zero_row = jnp.zeros(grads_ref.shape[2:], grads_ref.dtype)
            grads_ref[s, 0] = zero_row
            grads_ref[s, height + 1] = zero_row

    is_near = own_ref[frame] != 0
    message = jnp.where(is_near, near_ref[0].astype(jnp.float32), far_ref[0].astype(jnp.float32))
    mains = [message[k * height : (k + 1) * height] for k in range(3)]
    if rem > 0:
        tail = message[3 * height : 4 * height]
    for k in range(3):
        if rem > 0:
            line = jnp.concatenate([mains[k], tail[:, k * rem : (k + 1) * rem]], axis=1)
        else:
            line = mains[k]
        for s in range(3):
            for c in range(chunks):
                start = 3 - s + c * LANES
                stop = min(start + LANES, width + 4)
                part = line[:, start:stop]
                if stop - start < LANES:
                    blank = jnp.zeros((height, LANES - (stop - start)), jnp.float32)
                    part = jnp.concatenate([part, blank], axis=1)
                taps_ref[c, pl.ds(SUB + 3 * s + k, height, stride=SUB), :] = part
    pieces = mains + ([tail] if rem > 0 else [])
    wide = jnp.concatenate(pieces, axis=1).astype(jnp.bfloat16)
    per_tap = jnp.dot(wide, w_edge_ref[...], preferred_element_type=jnp.float32)
    zeros = jnp.zeros((1, 2 * LANES), jnp.float32)
    first, middle, last = (per_tap[:, i * 2 * LANES : (i + 1) * 2 * LANES] for i in range(3))
    edge = (
        jnp.concatenate([first[1:], zeros], axis=0)
        + middle
        + jnp.concatenate([zeros, last[: height - 1]], axis=0)
    )
    edge_ref[:, :LANES] = edge[:, :LANES] * silu_slope(left_ref[0].astype(jnp.float32))
    edge_ref[:, LANES:] = edge[:, LANES:] * silu_slope(right_ref[0].astype(jnp.float32))

    pairs = block_rows // 2

    def produce(block):
        base = block * block_rows
        lhs = jnp.concatenate(
            [
                taps_ref[c, (base + 2 * p) * SUB : (base + 2 * p + 4) * SUB, :]
                .T[: min(LANES, width - c * LANES)]
                .astype(jnp.bfloat16)
                for p in range(pairs)
                for c in range(chunks)
            ],
            axis=0,
        )
        back = jnp.dot(lhs, w_one_ref[...], preferred_element_type=jnp.float32)
        for i in range(block_rows):
            y = base + i
            p, h = i // 2, i % 2
            part = back[p * width : (p + 1) * width, h * LANES : (h + 1) * LANES]
            value = part * silu_slope(act_ref[0, y].astype(jnp.float32))
            slot = i % 4
            row_ref[slot, 8 : 8 + width, :] = value
            row_ref[slot, 7:8, :] = edge_ref[y : y + 1, :LANES]
            row_ref[slot, 8 + width : 9 + width, :] = edge_ref[y : y + 1, LANES:]
            grads_ref[0, y + 1] = row_ref[slot, 9 : 9 + width, :].astype(jnp.bfloat16)
            grads_ref[1, y + 1] = value.astype(jnp.bfloat16)
            grads_ref[2, y + 1] = row_ref[slot, 7 : 7 + width, :].astype(jnp.bfloat16)

    def consume(block):
        base = block * block_rows
        total = None
        slabs = []
        for j in range(4):
            for s in range(3):
                slabs.append(
                    jnp.concatenate([grads_ref[s, base + 2 * p + j] for p in range(pairs)], axis=0)
                )
        lhs = jnp.concatenate(slabs, axis=1)
        total = jnp.dot(lhs, w_two_ref[...], preferred_element_type=jnp.float32)
        for i in range(block_rows):
            p, h = i // 2, i % 2
            part = total[p * width : (p + 1) * width, h * LANES : (h + 1) * LANES]
            centre = grads_ref[1, base + i + 1].astype(jnp.float32)
            out_ref[0, base + i] = (part + centre).astype(out_ref.dtype)

    blocks = height // block_rows
    produce(0)
    for block in range(blocks):
        if block + 1 < blocks:
            produce(block + 1)
        consume(block)


def decoder_weights(conv_out_weight, conv_weight, height, width):
    rem = max(width + 4 - LANES, 0)
    taps_out = conv_out_weight.transpose(0, 1, 3, 2)
    channels = conv_weight.shape[2]
    small = jnp.pad(
        taps_out.reshape(3, 9, channels), ((0, 0), (0, SUB - 9), (0, 0))
    )
    none = jnp.zeros_like(small[0])
    w_one = jnp.concatenate(
        [
            jnp.stack([small[h - j + 2] if 0 <= h - j + 2 < 3 else none for j in range(4)])
            for h in range(2)
        ],
        axis=2,
    ).reshape(4 * SUB, 2 * channels)
    big = conv_weight.transpose(0, 1, 3, 2)
    none = jnp.zeros_like(big[0])
    w_two = jnp.concatenate(
        [
            jnp.stack([big[h - j + 2] if 0 <= h - j + 2 < 3 else none for j in range(4)])
            for h in range(2)
        ],
        axis=3,
    ).reshape(4 * 3 * channels, 2 * channels)
    flipped = taps_out[:, ::-1].transpose(0, 2, 1, 3)
    groups = 4 if rem > 0 else 3
    sides = []
    for r in range(3):
        left = jnp.zeros((groups * LANES, channels), conv_out_weight.dtype)
        right = jnp.zeros((groups * LANES, channels), conv_out_weight.dtype)
        for k in range(3):
            left = left.at[k * LANES : k * LANES + 3].set(flipped[r, k])
            for i in range(3):
                lane = width + 1 + i
                if lane < LANES:
                    place = k * LANES + lane
                else:
                    place = 3 * LANES + k * rem + lane - LANES
                right = right.at[place].set(flipped[r, k, i])
        sides.extend([left, right])
    w_edge = jnp.concatenate(sides, axis=1)
    return w_edge, w_one, w_two


def decode(pick, own, near, far, left, right, activations, conv_out_weight, conv_weight, block_rows):
    frames, height, width, channels = activations.shape
    rows = near.shape[1]
    w_edge, w_one, w_two = decoder_weights(conv_out_weight, conv_weight, height, width)
    whole = lambda shape: pl.BlockSpec(shape, lambda f, *_: (0,) * len(shape))
    padded = -(-(width + 9) // 8) * 8 + 8
    return pl.pallas_call(
        functools.partial(decoder_kernel, height, width, block_rows),
        out_shape=jax.ShapeDtypeStruct(activations.shape, jnp.bfloat16),
        grid_spec=pltpu.PrefetchScalarGridSpec(
            num_scalar_prefetch=2,
            grid=(frames,),
            in_specs=[
                pl.BlockSpec((1, rows, LANES), lambda f, pick, own: (pick[f], 0, 0)),
                pl.BlockSpec((1, rows, LANES), lambda f, pick, own: (f, 0, 0)),
                pl.BlockSpec((1, height, channels), lambda f, *_: (f, 0, 0)),
                pl.BlockSpec((1, height, channels), lambda f, *_: (f, 0, 0)),
                pl.BlockSpec((1, height, width, channels), lambda f, *_: (f, 0, 0, 0)),
                whole(w_edge.shape),
                whole(w_one.shape),
                whole(w_two.shape),
            ],
            out_specs=pl.BlockSpec((1, height, width, channels), lambda f, *_: (f, 0, 0, 0)),
            scratch_shapes=[
                pltpu.VMEM((-(-width // LANES), (height + 2) * SUB, LANES), jnp.float32),
                pltpu.VMEM((4, padded, channels), jnp.float32),
                pltpu.VMEM((height, 2 * channels), jnp.float32),
                pltpu.VMEM((3, height + 2, width, channels), jnp.bfloat16),
            ],
        ),
        compiler_params=pltpu.CompilerParams(vmem_limit_bytes=56 * 1024 * 1024),
        cost_estimate=pl.CostEstimate(
            flops=2 * frames * height * width * channels * (12 * channels + 64),
            bytes_accessed=4 * frames * height * width * channels,
            transcendentals=frames * height * width * channels,
        ),
    )(pick, own, near, far, left, right, activations, w_edge, w_one, w_two)


def dot(left, right, dims=((1,), (0,))):
    return lax.dot_general(left, right, (dims, ((), ())), preferred_element_type=WIDE)


def dot_rows(left, right):
    return dot(left, right, ((1,), (1,)))


def tower_kernel(
    tiles,
    pixel_ref,
    patch_ref,
    gain_ref,
    qkv_ref,
    proj_ref,
    post_gain_ref,
    text_ref,
    strip_ref,
    order_ref,
    patches_ref,
    unit_ref,
    scale_ref,
    normed_ref,
    heads_ref,
    head_scale_ref,
    probs_ref,
    column_ref,
    slope_ref,
    back_ref,
    grad_ref,
    tangent_ref,
):
    slots, colour_rows, columns = pixel_ref.shape
    height = colour_rows // 3
    dim = gain_ref.shape[1]
    across = columns // PATCH
    down = height // PATCH
    tokens = across * down
    bands = slots * down
    total = slots * tokens
    width = columns // tiles
    rem = max(width + 4 - LANES, 0)
    block = 2 * LANES

    column_id = lax.broadcasted_iota(jnp.int32, (columns, 1), 0)
    goal = (column_id % PATCH) * LANES + column_id // PATCH
    for j in range(PATCH):
        lane_id = lax.broadcasted_iota(jnp.int32, (columns, LANES), 1) + j * LANES
        order_ref[:, j * LANES : (j + 1) * LANES] = jnp.where(goal == lane_id, 1.0, 0.0).astype(
            NARROW
        )

    for f in range(slots):
        spread = dot(pixel_ref[f], order_ref[...])
        for py in range(down):
            entries = jnp.concatenate(
                [
                    spread[
                        k * height + py * PATCH : k * height + (py + 1) * PATCH,
                        j * LANES : (j + 1) * LANES,
                    ]
                    for j in range(PATCH)
                    for k in range(3)
                ],
                axis=0,
            )
            start = (f * down + py) * across
            patches_ref[start : start + across, :] = entries.T[:across].astype(NARROW)

    @pl.loop(0, dim // block)
    def _(n):
        at = pl.ds(pl.multiple_of(n * block, block), block)
        unit_ref[:, at] = dot(patches_ref[...], patch_ref[:, at])

    means = [jnp.zeros((1, dim), WIDE) for _ in range(slots)]
    for b in range(bands):
        rows = slice(b * across, (b + 1) * across)
        embedded = unit_ref[rows, :]
        means[b // down] += jnp.sum(embedded, axis=0, keepdims=True)
        centred = embedded - jnp.mean(embedded, axis=1, keepdims=True)
        scale = lax.rsqrt(jnp.mean(centred * centred, axis=1, keepdims=True) + EPS)
        unit = centred * scale
        unit_ref[rows, :] = unit
        scale_ref[rows, :] = jnp.broadcast_to(scale, (across, LANES))
        normed_ref[rows, :] = (unit * gain_ref[...]).astype(NARROW)
    means = [value * (1.0 / tokens) for value in means]

    row_head = lax.broadcasted_iota(jnp.int32, (LANES, LANES), 0) // HEAD_DIM
    lane_head = lax.broadcasted_iota(jnp.int32, (LANES, LANES), 1) // HEAD_DIM
    average = jnp.where(row_head == lane_head, 1.0 / HEAD_DIM, 0.0).astype(NARROW)

    @pl.loop(0, 2 * dim // block)
    def _(n):
        at = pl.multiple_of(n * block, block)
        both = dot(normed_ref[...], qkv_ref[:, pl.ds(at, block)])
        for i in range(2):
            part = both[:, i * LANES : (i + 1) * LANES]
            centred = part - dot(part.astype(NARROW), average)
            scale = lax.rsqrt(dot((centred * centred).astype(NARROW), average) + EPS)
            lanes = pl.ds(pl.multiple_of(at + i * LANES, LANES), LANES)
            head_scale_ref[:, lanes] = scale
            heads_ref[:, lanes] = (centred * scale).astype(NARROW)

    lane = lax.broadcasted_iota(jnp.int32, (1, LANES), 1)
    sides = [lane < HEAD_DIM, lane >= HEAD_DIM]
    factor = 1.0 / HEAD_DIM**0.5
    pairs = dim // LANES

    def pair_at(index):
        f = index // pairs
        i = index % pairs
        rows = pl.ds(pl.multiple_of(f * tokens, SUB), tokens)
        query_at = pl.ds(pl.multiple_of(i * LANES, LANES), LANES)
        key_at = pl.ds(pl.multiple_of(dim + i * LANES, LANES), LANES)
        return rows, query_at, key_at

    @pl.loop(0, slots * pairs)
    def _(index):
        rows, query_at, key_at = pair_at(index)
        query = heads_ref[rows, query_at]
        key = heads_ref[rows, key_at]
        for side in range(2):
            mask = jnp.where(sides[side], factor, 0.0).astype(NARROW)
            scores = dot_rows(query * mask, key)
            exps = jnp.exp(scores)
            probs = exps * (1.0 / jnp.sum(exps, axis=1, keepdims=True))
            column_ref[pl.ds(2 * index + side, 1), :] = jnp.sum(probs, axis=0, keepdims=True)
            probs_ref[2 * index + side] = probs.astype(NARROW)

    value_weight = qkv_ref.at[:, 2 * dim : 3 * dim]
    head_row = lax.broadcasted_iota(jnp.int32, (HEADS, dim), 0)
    head_lane = lax.broadcasted_iota(jnp.int32, (HEADS, dim), 1) // HEAD_DIM
    own_head = head_row == head_lane
    normed = [normed_ref[f * tokens : (f + 1) * tokens, :] for f in range(slots)]
    weights = [column_ref[f * HEADS : (f + 1) * HEADS, :].astype(NARROW) for f in range(slots)]
    mixed = jnp.concatenate([dot(weights[f], normed[f]) for f in range(slots)], axis=0)
    values = dot(mixed.astype(NARROW), value_weight[...])
    context = jnp.concatenate(
        [
            jnp.broadcast_to(
                jnp.sum(
                    jnp.where(own_head, values[f * HEADS : (f + 1) * HEADS], 0.0),
                    axis=0,
                    keepdims=True,
                )
                * (1.0 / tokens),
                (8, dim),
            )
            for f in range(slots)
        ],
        axis=0,
    )
    mean_rows = jnp.concatenate([jnp.broadcast_to(m, (8, dim)) for m in means], axis=0)
    pooled = mean_rows + dot(context.astype(NARROW), proj_ref[...])
    centred = pooled - jnp.mean(pooled, axis=1, keepdims=True)
    scale = lax.rsqrt(jnp.mean(centred * centred, axis=1, keepdims=True) + EPS)
    unit = centred * scale
    post = unit * post_gain_ref[...]
    text = text_ref[...]
    text = text * lax.rsqrt(jnp.sum(text * text, axis=1, keepdims=True) + EPS)
    along = jnp.sum(post * text, axis=1, keepdims=True)
    length = lax.rsqrt(jnp.sum(post * post, axis=1, keepdims=True) + EPS)
    post_back = (LOSS_SCALE * LOGIT_SCALE) * (length * text - along * length**3 * post)
    unit_back = post_back * post_gain_ref[...]
    pooled_back = scale * (
        unit_back
        - jnp.mean(unit_back, axis=1, keepdims=True)
        - unit * jnp.mean(unit_back * unit, axis=1, keepdims=True)
    )
    token_back = pooled_back * (1.0 / tokens)
    context_back = dot_rows(token_back.astype(NARROW), proj_ref[...])
    by_head = jnp.concatenate(
        [
            jnp.where(own_head, jnp.broadcast_to(context_back[8 * f : 8 * f + 1], (HEADS, dim)), 0.0)
            for f in range(slots)
        ],
        axis=0,
    )
    value_back = dot_rows(by_head.astype(NARROW), value_weight[...]).astype(NARROW)
    for f in range(slots):
        slope_ref[f * HEADS : (f + 1) * HEADS, :] = dot_rows(
            value_back[f * HEADS : (f + 1) * HEADS], normed[f]
        )

    def norm_back(gradient, rows, lanes):
        unit = heads_ref[rows, lanes].astype(WIDE)
        plain = dot(gradient.astype(NARROW), average)
        along = dot((gradient * unit).astype(NARROW), average)
        value = head_scale_ref[rows, lanes] * (gradient - plain - unit * along)
        back_ref[rows, lanes] = value.astype(NARROW)

    @pl.loop(0, slots * pairs)
    def _(index):
        rows, query_at, key_at = pair_at(index)
        query = heads_ref[rows, query_at]
        key = heads_ref[rows, key_at]
        query_back, key_back = [], []
        for side in range(2):
            probs = probs_ref[2 * index + side].astype(WIDE)
            slope = slope_ref[pl.ds(2 * index + side, 1), :]
            middle = jnp.sum(probs * slope, axis=1, keepdims=True)
            scores_back = (probs * (slope - middle) * factor).astype(NARROW)
            query_back.append(dot(scores_back, key))
            key_back.append(dot(scores_back, query, ((0,), (0,))))
        norm_back(jnp.where(sides[0], query_back[0], query_back[1]), rows, query_at)
        norm_back(jnp.where(sides[0], key_back[0], key_back[1]), rows, key_at)

    for f in range(slots):
        grad_ref[f * tokens : (f + 1) * tokens, :] = dot(
            weights[f], value_back[f * HEADS : (f + 1) * HEADS], ((0,), (0,))
        )

    @pl.loop(0, dim // block)
    def _(n):
        at = pl.ds(pl.multiple_of(n * block, block), block)
        grad_ref[:, at] += dot_rows(back_ref[...], qkv_ref[at, : 2 * dim])

    tangent_ref[...] = jnp.zeros_like(tangent_ref)
    for b in range(bands):
        rows = slice(b * across, (b + 1) * across)
        f = b // down
        unit = unit_ref[rows, :]
        unit_back = grad_ref[rows, :] * gain_ref[...]
        value = (
            unit_back
            - jnp.mean(unit_back, axis=1, keepdims=True)
            - unit * jnp.mean(unit_back * unit, axis=1, keepdims=True)
        )
        value = scale_ref[rows, :1] * value + token_back[8 * f : 8 * f + 1]
        tangent_ref[b * LANES : b * LANES + across, :] = value.astype(NARROW)

    for f in range(slots):
        entries = dot_rows(
            patch_ref[...], tangent_ref[f * down * LANES : (f + 1) * down * LANES, :]
        ).astype(NARROW)
        lines = []
        for k in range(3):
            for py in range(down):
                lines.append(
                    jnp.concatenate(
                        [
                            entries[
                                (3 * j + k) * PATCH : (3 * j + k + 1) * PATCH,
                                py * LANES : (py + 1) * LANES,
                            ]
                            for j in range(PATCH)
                        ],
                        axis=1,
                    )
                )
        frame = dot_rows(jnp.concatenate(lines, axis=0), order_ref[...])
        frame = jnp.concatenate(
            [
                jnp.zeros((colour_rows, 2), WIDE),
                frame,
                jnp.zeros((colour_rows, LANES - 2), WIDE),
            ],
            axis=1,
        )
        for t in range(tiles):
            base = t * width
            main = frame[:, base : base + LANES]
            if rem == 0 and width + 4 < LANES:
                main = jnp.where(lane < width + 4, main, 0.0)
            strip_ref[t, f, :colour_rows, :] = main.astype(NARROW)
            if rem > 0:
                tail = [
                    frame[
                        k * height : (k + 1) * height, base + LANES : base + LANES + rem
                    ]
                    for k in range(3)
                ]
                tail.append(jnp.zeros((height, LANES - 3 * rem), WIDE))
                strip_ref[t, f, colour_rows:, :] = jnp.concatenate(tail, axis=1).astype(NARROW)


def tower(
    pixels, patch_weight, norm_gain, qkv_weight, out_weight, post_gain, text_embed, tiles
):
    slots, colours, height, columns = pixels.shape
    dim = norm_gain.shape[0]
    across = columns // PATCH
    down = height // PATCH
    tokens = across * down
    total = slots * tokens
    width = columns // tiles
    rows = colours * height + (height if width + 4 > LANES else 0)
    entries = colours * PATCH * PATCH
    reordered = (
        patch_weight.reshape(colours * PATCH, PATCH, dim).transpose(1, 0, 2).reshape(entries, dim)
    )
    vmem = pl.BlockSpec(memory_space=pltpu.VMEM)
    return pl.pallas_call(
        functools.partial(tower_kernel, tiles),
        out_shape=jax.ShapeDtypeStruct((tiles, slots, rows, LANES), NARROW),
        in_specs=[vmem] * 7,
        out_specs=vmem,
        scratch_shapes=[
            pltpu.VMEM((columns, PATCH * LANES), NARROW),
            pltpu.VMEM((total, entries), NARROW),
            pltpu.VMEM((total, dim), WIDE),
            pltpu.VMEM((total, LANES), WIDE),
            pltpu.VMEM((total, dim), NARROW),
            pltpu.VMEM((total, 2 * dim), NARROW),
            pltpu.VMEM((total, 2 * dim), WIDE),
            pltpu.VMEM((slots * HEADS, tokens, tokens), NARROW),
            pltpu.VMEM((slots * HEADS, tokens), WIDE),
            pltpu.VMEM((slots * HEADS, tokens), WIDE),
            pltpu.VMEM((total, 2 * dim), NARROW),
            pltpu.VMEM((total, dim), WIDE),
            pltpu.VMEM((slots * down * LANES, dim), NARROW),
        ],
        compiler_params=pltpu.CompilerParams(vmem_limit_bytes=60 * 1024 * 1024),
        cost_estimate=pl.CostEstimate(
            flops=2 * total * dim * (2 * entries + 4 * dim + 4 * tokens),
            bytes_accessed=2 * (entries * dim + 4 * dim * dim),
            transcendentals=slots * HEADS * tokens * tokens,
        ),
    )(
        pixels.reshape(slots, colours * height, columns),
        reordered,
        norm_gain[None],
        qkv_weight,
        out_weight,
        post_gain[None],
        text_embed[None],
    )


def frame_rank(owner):
    frame_ids = jnp.arange(owner.shape[0], dtype=jnp.int32)
    same_owner = owner[:, None] == owner[None, :]
    earlier = frame_ids[None, :] < frame_ids[:, None]
    return jnp.sum((same_owner & earlier).astype(jnp.int32), axis=1)


def local(
    pixels,
    owner,
    patch_weight,
    norm_gain,
    qkv_weight,
    out_weight,
    post_gain,
    text_embed,
    conv_out_weight,
    conv_weight,
    activations,
):
    tile_count = lax.axis_size("tile")
    core_count = lax.axis_size("tm")
    core = lax.axis_index("tm")
    tile = lax.axis_index("tile")
    frames, height, width, channels = activations.shape
    slots = pixels.shape[0]
    ranks_all = frame_rank(owner)

    up = [(i, i + 1) for i in range(tile_count - 1)]
    down = [(j, i) for i, j in up]
    outside = jnp.asarray(-30000.0, activations.dtype)
    left = lax.ppermute(activations[:, :, width - 1], "tile", up)
    right = lax.ppermute(activations[:, :, 0], "tile", down)
    left = jnp.where(tile == 0, outside, left)
    right = jnp.where(tile == tile_count - 1, outside, right)

    outgoing = tower(
        pixels, patch_weight, norm_gain, qkv_weight, out_weight, post_gain, text_embed, tile_count
    )
    rows = outgoing.shape[2]
    near = lax.all_to_all(outgoing, "tile", split_axis=0, concat_axis=0, tiled=True)
    near = near.reshape(tile_count * slots, rows, LANES)
    pick_all = (owner // core_count) * slots + ranks_all
    own_all = owner % core_count
    by_core = lambda values, index: lax.dynamic_slice_in_dim(values, index * frames, frames)
    other = 1 - core
    far = lax.ppermute(jnp.take(near, by_core(pick_all, other), axis=0), "tm", [(0, 1), (1, 0)])
    return decode(
        by_core(pick_all, core),
        (by_core(own_all, core) == core).astype(jnp.int32),
        near,
        far,
        left,
        right,
        activations,
        conv_out_weight,
        conv_weight,
        4,
    )


def solution(mesh):
    placed = (
        P(("groups", "tile", "tm"), None, None, None),
        P("groups"),
        P(),
        P(),
        P(),
        P(),
        P(),
        P("groups"),
        P(),
        P(),
        P(("groups", "tm"), None, "tile", None),
    )
    return jax.shard_map(
        local,
        mesh=mesh,
        in_specs=placed,
        out_specs=P(("groups", "tm"), None, "tile", None),
        check_vma=False,
    )
```

```python
import functools

import jax
import jax.numpy as jnp
from jax import lax
from jax.experimental import pallas as pl
from jax.experimental.pallas import tpu as pltpu
from jax.sharding import PartitionSpec as P

HEADS = 16
HEAD_DIM = 64
PATCH = 16
EPS = 1e-06
LOGIT_SCALE = 100.0
LOSS_SCALE = 64.0

LANES = 128
SUB = 16
NARROW = jnp.bfloat16
WIDE = jnp.float32


def silu_slope(pre_value):
    half = 0.5 * pre_value
    gate = jnp.tanh(half)
    return (1.0 + gate) * (1.0 + half * (1.0 - gate))


def decoder_kernel(
    height,
    width,
    block_rows,
    pick_ref,
    own_ref,
    near_ref,
    far_ref,
    left_ref,
    right_ref,
    act_ref,
    w_edge_ref,
    w_one_ref,
    w_two_ref,
    out_ref,
    taps_ref,
    row_ref,
    edge_ref,
    grads_ref,
):
    frame = pl.program_id(0)
    rem = max(width + 4 - LANES, 0)
    chunks = -(-width // LANES)

    @pl.when(frame == 0)
    def _():
        taps_ref[...] = jnp.zeros_like(taps_ref)
        for s in range(3):
            zero_row = jnp.zeros(grads_ref.shape[2:], grads_ref.dtype)
            grads_ref[s, 0] = zero_row
            grads_ref[s, height + 1] = zero_row

    is_near = own_ref[frame] != 0
    message = jnp.where(is_near, near_ref[0].astype(jnp.float32), far_ref[0].astype(jnp.float32))
    mains = [message[k * height : (k + 1) * height] for k in range(3)]
    if rem > 0:
        tail = message[3 * height : 4 * height]
    for k in range(3):
        if rem > 0:
            line = jnp.concatenate([mains[k], tail[:, k * rem : (k + 1) * rem]], axis=1)
        else:
            line = mains[k]
        for s in range(3):
            for c in range(chunks):
                start = 3 - s + c * LANES
                stop = min(start + LANES, width + 4)
                part = line[:, start:stop]
                if stop - start < LANES:
                    blank = jnp.zeros((height, LANES - (stop - start)), jnp.float32)
                    part = jnp.concatenate([part, blank], axis=1)
                taps_ref[c, pl.ds(SUB + 3 * s + k, height, stride=SUB), :] = part
    pieces = mains + ([tail] if rem > 0 else [])
    wide = jnp.concatenate(pieces, axis=1).astype(jnp.bfloat16)
    per_tap = jnp.dot(wide, w_edge_ref[...], preferred_element_type=jnp.float32)
    zeros = jnp.zeros((1, 2 * LANES), jnp.float32)
    first, middle, last = (per_tap[:, i * 2 * LANES : (i + 1) * 2 * LANES] for i in range(3))
    edge = (
        jnp.concatenate([first[1:], zeros], axis=0)
        + middle
        + jnp.concatenate([zeros, last[: height - 1]], axis=0)
    )
    edge_ref[:, :LANES] = edge[:, :LANES] * silu_slope(left_ref[0].astype(jnp.float32))
    edge_ref[:, LANES:] = edge[:, LANES:] * silu_slope(right_ref[0].astype(jnp.float32))

    pairs = block_rows // 2

    def produce(block):
        base = block * block_rows
        lhs = jnp.concatenate(
            [
                taps_ref[c, (base + 2 * p) * SUB : (base + 2 * p + 4) * SUB, :]
                .T[: min(LANES, width - c * LANES)]
                .astype(jnp.bfloat16)
                for p in range(pairs)
                for c in range(chunks)
            ],
            axis=0,
        )
        back = jnp.dot(lhs, w_one_ref[...], preferred_element_type=jnp.float32)
        for i in range(block_rows):
            y = base + i
            p, h = i // 2, i % 2
            part = back[p * width : (p + 1) * width, h * LANES : (h + 1) * LANES]
            value = part * silu_slope(act_ref[0, y].astype(jnp.float32))
            slot = i % 4
            row_ref[slot, 8 : 8 + width, :] = value
            row_ref[slot, 7:8, :] = edge_ref[y : y + 1, :LANES]
            row_ref[slot, 8 + width : 9 + width, :] = edge_ref[y : y + 1, LANES:]
            grads_ref[0, y + 1] = row_ref[slot, 9 : 9 + width, :].astype(jnp.bfloat16)
            grads_ref[1, y + 1] = value.astype(jnp.bfloat16)
            grads_ref[2, y + 1] = row_ref[slot, 7 : 7 + width, :].astype(jnp.bfloat16)

    def consume(block):
        base = block * block_rows
        total = None
        slabs = []
        for j in range(4):
            for s in range(3):
                slabs.append(
                    jnp.concatenate([grads_ref[s, base + 2 * p + j] for p in range(pairs)], axis=0)
                )
        lhs = jnp.concatenate(slabs, axis=1)
        total = jnp.dot(lhs, w_two_ref[...], preferred_element_type=jnp.float32)
        for i in range(block_rows):
            p, h = i // 2, i % 2
            part = total[p * width : (p + 1) * width, h * LANES : (h + 1) * LANES]
            centre = grads_ref[1, base + i + 1].astype(jnp.float32)
            out_ref[0, base + i] = (part + centre).astype(out_ref.dtype)

    blocks = height // block_rows
    produce(0)
    for block in range(blocks):
        if block + 1 < blocks:
            produce(block + 1)
        consume(block)


def decoder_weights(conv_out_weight, conv_weight, height, width):
    rem = max(width + 4 - LANES, 0)
    taps_out = 0.5 * conv_out_weight.transpose(0, 1, 3, 2)
    channels = conv_weight.shape[2]
    small = jnp.pad(
        taps_out.reshape(3, 9, channels), ((0, 0), (0, SUB - 9), (0, 0))
    )
    none = jnp.zeros_like(small[0])
    w_one = jnp.concatenate(
        [
            jnp.stack([small[h - j + 2] if 0 <= h - j + 2 < 3 else none for j in range(4)])
            for h in range(2)
        ],
        axis=2,
    ).reshape(4 * SUB, 2 * channels)
    big = conv_weight.transpose(0, 1, 3, 2)
    none = jnp.zeros_like(big[0])
    w_two = jnp.concatenate(
        [
            jnp.stack([big[h - j + 2] if 0 <= h - j + 2 < 3 else none for j in range(4)])
            for h in range(2)
        ],
        axis=3,
    ).reshape(4 * 3 * channels, 2 * channels)
    flipped = taps_out[:, ::-1].transpose(0, 2, 1, 3)
    groups = 4 if rem > 0 else 3
    sides = []
    for r in range(3):
        left = jnp.zeros((groups * LANES, channels), conv_out_weight.dtype)
        right = jnp.zeros((groups * LANES, channels), conv_out_weight.dtype)
        for k in range(3):
            left = left.at[k * LANES : k * LANES + 3].set(flipped[r, k])
            for i in range(3):
                lane = width + 1 + i
                if lane < LANES:
                    place = k * LANES + lane
                else:
                    place = 3 * LANES + k * rem + lane - LANES
                right = right.at[place].set(flipped[r, k, i])
        sides.extend([left, right])
    w_edge = jnp.concatenate(sides, axis=1)
    return w_edge, w_one, w_two


def decode(pick, own, near, far, left, right, activations, conv_out_weight, conv_weight, block_rows):
    frames, height, width, channels = activations.shape
    rows = near.shape[1]
    w_edge, w_one, w_two = decoder_weights(conv_out_weight, conv_weight, height, width)
    whole = lambda shape: pl.BlockSpec(shape, lambda f, *_: (0,) * len(shape))
    padded = -(-(width + 9) // 8) * 8 + 8
    return pl.pallas_call(
        functools.partial(decoder_kernel, height, width, block_rows),
        out_shape=jax.ShapeDtypeStruct(activations.shape, jnp.bfloat16),
        grid_spec=pltpu.PrefetchScalarGridSpec(
            num_scalar_prefetch=2,
            grid=(frames,),
            in_specs=[
                pl.BlockSpec((1, rows, LANES), lambda f, pick, own: (pick[f], 0, 0)),
                pl.BlockSpec((1, rows, LANES), lambda f, pick, own: (f, 0, 0)),
                pl.BlockSpec((1, height, channels), lambda f, *_: (f, 0, 0)),
                pl.BlockSpec((1, height, channels), lambda f, *_: (f, 0, 0)),
                pl.BlockSpec((1, height, width, channels), lambda f, *_: (f, 0, 0, 0)),
                whole(w_edge.shape),
                whole(w_one.shape),
                whole(w_two.shape),
            ],
            out_specs=pl.BlockSpec((1, height, width, channels), lambda f, *_: (f, 0, 0, 0)),
            scratch_shapes=[
                pltpu.VMEM((-(-width // LANES), (height + 2) * SUB, LANES), jnp.float32),
                pltpu.VMEM((4, padded, channels), jnp.float32),
                pltpu.VMEM((height, 2 * channels), jnp.float32),
                pltpu.VMEM((3, height + 2, width, channels), jnp.bfloat16),
            ],
        ),
        compiler_params=pltpu.CompilerParams(vmem_limit_bytes=56 * 1024 * 1024),
        cost_estimate=pl.CostEstimate(
            flops=2 * frames * height * width * channels * (12 * channels + 64),
            bytes_accessed=4 * frames * height * width * channels,
            transcendentals=frames * height * width * channels,
        ),
    )(pick, own, near, far, left, right, activations, w_edge, w_one, w_two)


def dot(left, right, dims=((1,), (0,))):
    return lax.dot_general(left, right, (dims, ((), ())), preferred_element_type=WIDE)


def dot_rows(left, right):
    return dot(left, right, ((1,), (1,)))


def tower_kernel(
    tiles,
    pixel_ref,
    patch_raw_ref,
    gain_ref,
    qkv_ref,
    proj_ref,
    post_gain_ref,
    text_ref,
    strip_ref,
    order_ref,
    patches_ref,
    unit_ref,
    scale_ref,
    normed_ref,
    heads_ref,
    head_scale_ref,
    probs_ref,
    column_ref,
    slope_ref,
    back_ref,
    grad_ref,
    tangent_ref,
    qkv_copy_ref,
    proj_copy_ref,
    patch_order_ref,
    sems,
):
    qkv_copy = pltpu.make_async_copy(qkv_ref, qkv_copy_ref, sems.at[0])
    proj_copy = pltpu.make_async_copy(proj_ref, proj_copy_ref, sems.at[1])
    qkv_copy.start()
    proj_copy.start()
    slots, colour_rows, columns = pixel_ref.shape
    height = colour_rows // 3
    dim = gain_ref.shape[1]
    across = columns // PATCH
    down = height // PATCH
    tokens = across * down
    bands = slots * down
    total = slots * tokens
    width = columns // tiles
    rem = max(width + 4 - LANES, 0)
    block = 2 * LANES

    column_id = lax.broadcasted_iota(jnp.int32, (columns, 1), 0)
    goal = (column_id % PATCH) * LANES + column_id // PATCH
    for j in range(PATCH):
        lane_id = lax.broadcasted_iota(jnp.int32, (columns, LANES), 1) + j * LANES
        order_ref[:, j * LANES : (j + 1) * LANES] = jnp.where(goal == lane_id, 1.0, 0.0).astype(
            NARROW
        )

    entries_count = patch_raw_ref.shape[0]
    row_id = lax.broadcasted_iota(jnp.int32, (entries_count, 1), 0)
    lines_count = entries_count // PATCH
    goal = (row_id % lines_count) * PATCH + row_id // lines_count
    entry_id = lax.broadcasted_iota(jnp.int32, (entries_count, entries_count), 1)
    move = jnp.where(goal == entry_id, 1.0, 0.0).astype(NARROW)
    patch_ref = patch_order_ref
    for n in range(dim // block):
        at = slice(n * block, (n + 1) * block)
        patch_ref[:, at] = dot(move, patch_raw_ref[:, at]).astype(NARROW)

    for f in range(slots):
        spread = dot(pixel_ref[f], order_ref[...])
        for py in range(down):
            entries = jnp.concatenate(
                [
                    spread[
                        k * height + py * PATCH : k * height + (py + 1) * PATCH,
                        j * LANES : (j + 1) * LANES,
                    ]
                    for j in range(PATCH)
                    for k in range(3)
                ],
                axis=0,
            )
            start = (f * down + py) * across
            patches_ref[start : start + across, :] = entries.T[:across].astype(NARROW)

    @pl.loop(0, dim // block, unroll=2)
    def _(n):
        at = pl.ds(pl.multiple_of(n * block, block), block)
        unit_ref[:, at] = dot(patches_ref[...], patch_ref[:, at])

    means = [jnp.zeros((1, dim), WIDE) for _ in range(slots)]
    for b in range(bands):
        rows = slice(b * across, (b + 1) * across)
        embedded = unit_ref[rows, :]
        means[b // down] += jnp.sum(embedded, axis=0, keepdims=True)
        centred = embedded - jnp.mean(embedded, axis=1, keepdims=True)
        scale = lax.rsqrt(jnp.mean(centred * centred, axis=1, keepdims=True) + EPS)
        unit = centred * scale
        unit_ref[rows, :] = unit
        scale_ref[rows, :] = jnp.broadcast_to(scale, (across, LANES))
        normed_ref[rows, :] = (unit * gain_ref[...]).astype(NARROW)
    means = [value * (1.0 / tokens) for value in means]

    qkv_copy.wait()
    proj_copy.wait()
    qkv_ref, proj_ref = qkv_copy_ref, proj_copy_ref

    row_head = lax.broadcasted_iota(jnp.int32, (block, block), 0) // HEAD_DIM
    lane_head = lax.broadcasted_iota(jnp.int32, (block, block), 1) // HEAD_DIM
    average = jnp.where(row_head == lane_head, 1.0 / HEAD_DIM, 0.0).astype(NARROW)

    @pl.loop(0, 2 * dim // block)
    def _(n):
        at = pl.multiple_of(n * block, block)
        both = dot(normed_ref[...], qkv_ref[:, pl.ds(at, block)])
        centred = both - dot(both.astype(NARROW), average)
        scale = lax.rsqrt(dot((centred * centred).astype(NARROW), average) + EPS)
        head_scale_ref[:, pl.ds(at, block)] = scale
        heads_ref[:, pl.ds(at, block)] = (centred * scale).astype(NARROW)

    lane = lax.broadcasted_iota(jnp.int32, (1, LANES), 1)
    sides = [lane < HEAD_DIM, lane >= HEAD_DIM]
    factor = 1.0 / HEAD_DIM**0.5
    pairs = dim // LANES

    def pair_at(index):
        f = index // pairs
        i = index % pairs
        rows = pl.ds(pl.multiple_of(f * tokens, SUB), tokens)
        query_at = pl.ds(pl.multiple_of(i * LANES, LANES), LANES)
        key_at = pl.ds(pl.multiple_of(dim + i * LANES, LANES), LANES)
        return rows, query_at, key_at

    @pl.loop(0, slots * pairs, unroll=16)
    def _(index):
        rows, query_at, key_at = pair_at(index)
        query = heads_ref[rows, query_at]
        key = heads_ref[rows, key_at]
        for side in range(2):
            mask = jnp.where(sides[side], factor, 0.0).astype(NARROW)
            scores = dot_rows(query * mask, key)
            exps = jnp.exp(scores)
            probs = exps * (1.0 / jnp.sum(exps, axis=1, keepdims=True))
            column_ref[pl.ds(2 * index + side, 1), :] = jnp.sum(probs, axis=0, keepdims=True)
            probs_ref[2 * index + side] = probs.astype(NARROW)

    value_weight = qkv_ref.at[:, 2 * dim : 3 * dim]
    head_row = lax.broadcasted_iota(jnp.int32, (HEADS, dim), 0)
    head_lane = lax.broadcasted_iota(jnp.int32, (HEADS, dim), 1) // HEAD_DIM
    own_head = head_row == head_lane
    normed = [normed_ref[f * tokens : (f + 1) * tokens, :] for f in range(slots)]
    weights = [column_ref[f * HEADS : (f + 1) * HEADS, :].astype(NARROW) for f in range(slots)]
    mixed = jnp.concatenate([dot(weights[f], normed[f]) for f in range(slots)], axis=0)
    values = dot(mixed.astype(NARROW), value_weight[...])
    context = jnp.concatenate(
        [
            jnp.broadcast_to(
                jnp.sum(
                    jnp.where(own_head, values[f * HEADS : (f + 1) * HEADS], 0.0),
                    axis=0,
                    keepdims=True,
                )
                * (1.0 / tokens),
                (8, dim),
            )
            for f in range(slots)
        ],
        axis=0,
    )
    mean_rows = jnp.concatenate([jnp.broadcast_to(m, (8, dim)) for m in means], axis=0)
    pooled = mean_rows + dot(context.astype(NARROW), proj_ref[...])
    centred = pooled - jnp.mean(pooled, axis=1, keepdims=True)
    scale = lax.rsqrt(jnp.mean(centred * centred, axis=1, keepdims=True) + EPS)
    unit = centred * scale
    post = unit * post_gain_ref[...]
    text = text_ref[...]
    text = text * lax.rsqrt(jnp.sum(text * text, axis=1, keepdims=True) + EPS)
    along = jnp.sum(post * text, axis=1, keepdims=True)
    length = lax.rsqrt(jnp.sum(post * post, axis=1, keepdims=True) + EPS)
    post_back = (LOSS_SCALE * LOGIT_SCALE) * (length * text - along * length**3 * post)
    unit_back = post_back * post_gain_ref[...]
    pooled_back = scale * (
        unit_back
        - jnp.mean(unit_back, axis=1, keepdims=True)
        - unit * jnp.mean(unit_back * unit, axis=1, keepdims=True)
    )
    token_back = pooled_back * (1.0 / tokens)
    context_back = dot_rows(token_back.astype(NARROW), proj_ref[...])
    by_head = jnp.concatenate(
        [
            jnp.where(own_head, jnp.broadcast_to(context_back[8 * f : 8 * f + 1], (HEADS, dim)), 0.0)
            for f in range(slots)
        ],
        axis=0,
    )
    value_back = dot_rows(by_head.astype(NARROW), value_weight[...]).astype(NARROW)
    for f in range(slots):
        slope_ref[f * HEADS : (f + 1) * HEADS, :] = dot_rows(
            value_back[f * HEADS : (f + 1) * HEADS], normed[f]
        )

    @pl.loop(0, slots * pairs, unroll=16)
    def _(index):
        rows, query_at, key_at = pair_at(index)
        query = heads_ref[rows, query_at]
        key = heads_ref[rows, key_at]
        query_back, key_back = [], []
        for side in range(2):
            probs = probs_ref[2 * index + side].astype(WIDE)
            slope = slope_ref[pl.ds(2 * index + side, 1), :]
            middle = jnp.sum(probs * slope, axis=1, keepdims=True)
            scores_back = (probs * (slope - middle)).astype(NARROW)
            query_back.append(dot(scores_back, key))
            key_back.append(dot(scores_back, query, ((0,), (0,))))
        gradient = jnp.concatenate(
            [
                jnp.where(sides[0], query_back[0], query_back[1]),
                jnp.where(sides[0], key_back[0], key_back[1]),
            ],
            axis=1,
        )
        unit = jnp.concatenate([query, key], axis=1).astype(WIDE)
        plain = dot(gradient.astype(NARROW), average)
        along = dot((gradient * unit).astype(NARROW), average)
        value = factor * (gradient - plain - unit * along)
        back_ref[rows, query_at] = (head_scale_ref[rows, query_at] * value[:, :LANES]).astype(NARROW)
        back_ref[rows, key_at] = (head_scale_ref[rows, key_at] * value[:, LANES:]).astype(NARROW)

    for f in range(slots):
        grad_ref[f * tokens : (f + 1) * tokens, :] = dot(
            weights[f], value_back[f * HEADS : (f + 1) * HEADS], ((0,), (0,))
        )

    @pl.loop(0, dim // block, unroll=2)
    def _(n):
        at = pl.ds(pl.multiple_of(n * block, block), block)
        grad_ref[:, at] += dot_rows(back_ref[...], qkv_ref[at, : 2 * dim])

    tangent_ref[...] = jnp.zeros_like(tangent_ref)
    for b in range(bands):
        rows = slice(b * across, (b + 1) * across)
        f = b // down
        unit = unit_ref[rows, :]
        unit_back = grad_ref[rows, :] * gain_ref[...]
        value = (
            unit_back
            - jnp.mean(unit_back, axis=1, keepdims=True)
            - unit * jnp.mean(unit_back * unit, axis=1, keepdims=True)
        )
        value = scale_ref[rows, :1] * value + token_back[8 * f : 8 * f + 1]
        tangent_ref[b * LANES : b * LANES + across, :] = value.astype(NARROW)

    for f in range(slots):
        entries = dot_rows(
            patch_ref[...], tangent_ref[f * down * LANES : (f + 1) * down * LANES, :]
        ).astype(NARROW)
        lines = []
        for k in range(3):
            for py in range(down):
                lines.append(
                    jnp.concatenate(
                        [
                            entries[
                                (3 * j + k) * PATCH : (3 * j + k + 1) * PATCH,
                                py * LANES : (py + 1) * LANES,
                            ]
                            for j in range(PATCH)
                        ],
                        axis=1,
                    )
                )
        frame = dot_rows(jnp.concatenate(lines, axis=0), order_ref[...])
        frame = jnp.concatenate(
            [
                jnp.zeros((colour_rows, 2), WIDE),
                frame,
                jnp.zeros((colour_rows, LANES - 2), WIDE),
            ],
            axis=1,
        )
        for t in range(tiles):
            base = t * width
            main = frame[:, base : base + LANES]
            if rem == 0 and width + 4 < LANES:
                main = jnp.where(lane < width + 4, main, 0.0)
            strip_ref[t, f, :colour_rows, :] = main.astype(NARROW)
            if rem > 0:
                tail = [
                    frame[
                        k * height : (k + 1) * height, base + LANES : base + LANES + rem
                    ]
                    for k in range(3)
                ]
                tail.append(jnp.zeros((height, LANES - 3 * rem), WIDE))
                strip_ref[t, f, colour_rows:, :] = jnp.concatenate(tail, axis=1).astype(NARROW)


def tower(
    pixels, patch_weight, norm_gain, qkv_weight, out_weight, post_gain, text_embed, tiles
):
    slots, colours, height, columns = pixels.shape
    dim = norm_gain.shape[0]
    across = columns // PATCH
    down = height // PATCH
    tokens = across * down
    total = slots * tokens
    width = columns // tiles
    rows = colours * height + (height if width + 4 > LANES else 0)
    entries = colours * PATCH * PATCH
    vmem = pl.BlockSpec(memory_space=pltpu.VMEM)
    return pl.pallas_call(
        functools.partial(tower_kernel, tiles),
        out_shape=jax.ShapeDtypeStruct((tiles, slots, rows, LANES), NARROW),
        in_specs=[vmem] * 3 + [pl.BlockSpec(memory_space=pl.ANY)] * 2 + [vmem] * 2,
        out_specs=vmem,
        scratch_shapes=[
            pltpu.VMEM((columns, PATCH * LANES), NARROW),
            pltpu.VMEM((total, entries), NARROW),
            pltpu.VMEM((total, dim), WIDE),
            pltpu.VMEM((total, LANES), WIDE),
            pltpu.VMEM((total, dim), NARROW),
            pltpu.VMEM((total, 2 * dim), NARROW),
            pltpu.VMEM((total, 2 * dim), WIDE),
            pltpu.VMEM((slots * HEADS, tokens, tokens), NARROW),
            pltpu.VMEM((slots * HEADS, tokens), WIDE),
            pltpu.VMEM((slots * HEADS, tokens), WIDE),
            pltpu.VMEM((total, 2 * dim), NARROW),
            pltpu.VMEM((total, dim), WIDE),
            pltpu.VMEM((slots * down * LANES, dim), NARROW),
            pltpu.VMEM(qkv_weight.shape, NARROW),
            pltpu.VMEM(out_weight.shape, NARROW),
            pltpu.VMEM((entries, dim), NARROW),
            pltpu.SemaphoreType.DMA((2,)),
        ],
        compiler_params=pltpu.CompilerParams(vmem_limit_bytes=60 * 1024 * 1024),
        cost_estimate=pl.CostEstimate(
            flops=2 * total * dim * (2 * entries + 4 * dim + 4 * tokens),
            bytes_accessed=2 * (entries * dim + 4 * dim * dim),
            transcendentals=slots * HEADS * tokens * tokens,
        ),
    )(
        pixels.reshape(slots, colours * height, columns),
        patch_weight,
        norm_gain[None],
        qkv_weight,
        out_weight,
        post_gain[None],
        text_embed[None],
    )


def frame_rank(owner):
    frame_ids = jnp.arange(owner.shape[0], dtype=jnp.int32)
    same_owner = owner[:, None] == owner[None, :]
    earlier = frame_ids[None, :] < frame_ids[:, None]
    return jnp.sum((same_owner & earlier).astype(jnp.int32), axis=1)


def local(
    pixels,
    owner,
    patch_weight,
    norm_gain,
    qkv_weight,
    out_weight,
    post_gain,
    text_embed,
    conv_out_weight,
    conv_weight,
    activations,
):
    tile_count = lax.axis_size("tile")
    core_count = lax.axis_size("tm")
    core = lax.axis_index("tm")
    tile = lax.axis_index("tile")
    frames, height, width, channels = activations.shape
    slots = pixels.shape[0]
    ranks_all = frame_rank(owner)

    outgoing = tower(
        pixels, patch_weight, norm_gain, qkv_weight, out_weight, post_gain, text_embed, tile_count
    )
    outgoing, origin = lax.optimization_barrier((outgoing, jnp.int32(0)))
    rows = outgoing.shape[2]
    near = lax.all_to_all(outgoing, "tile", split_axis=0, concat_axis=0, tiled=True)
    up = [(i, i + 1) for i in range(tile_count - 1)]
    down = [(j, i) for i, j in up]
    outside = jnp.asarray(-30000.0, activations.dtype)
    left = lax.ppermute(lax.dynamic_index_in_dim(activations, origin + (width - 1), 2, False), "tile", up)
    right = lax.ppermute(lax.dynamic_index_in_dim(activations, origin, 2, False), "tile", down)
    left = jnp.where(tile == 0, outside, left)
    right = jnp.where(tile == tile_count - 1, outside, right)

    near = near.reshape(tile_count * slots, rows, LANES)
    pick_all = (owner // core_count) * slots + ranks_all
    own_all = owner % core_count
    by_core = lambda values, index: lax.dynamic_slice_in_dim(values, index * frames, frames)
    other = 1 - core
    far = lax.ppermute(jnp.take(near, by_core(pick_all, other), axis=0), "tm", [(0, 1), (1, 0)])
    return decode(
        by_core(pick_all, core),
        (by_core(own_all, core) == core).astype(jnp.int32),
        near,
        far,
        left,
        right,
        activations,
        conv_out_weight,
        conv_weight,
        4,
    )


def solution(mesh):
    placed = (
        P(("groups", "tile", "tm"), None, None, None),
        P("groups"),
        P(),
        P(),
        P(),
        P(),
        P(),
        P("groups"),
        P(),
        P(),
        P(("groups", "tm"), None, "tile", None),
    )
    return jax.shard_map(
        local,
        mesh=mesh,
        in_specs=placed,
        out_specs=P(("groups", "tm"), None, "tile", None),
        check_vma=False,
    )
```

```python
import functools

import jax
import jax.numpy as jnp
from jax import lax
from jax.experimental import pallas as pl
from jax.experimental.pallas import tpu as pltpu
from jax.sharding import PartitionSpec as P

HEADS = 16
HEAD_DIM = 64
PATCH = 16
EPS = 1e-06
LOGIT_SCALE = 100.0
LOSS_SCALE = 64.0

LANES = 128
SUB = 16
NARROW = jnp.bfloat16
WIDE = jnp.float32


def silu_slope(pre_value):
    half = 0.5 * pre_value
    gate = jnp.tanh(half)
    return (1.0 + gate) * (1.0 + half * (1.0 - gate))


def decoder_kernel(
    height,
    width,
    block_rows,
    code_ref,
    near_ref,
    far_ref,
    left_ref,
    right_ref,
    act_ref,
    w_edge_ref,
    w_one_ref,
    w_two_ref,
    out_ref,
    taps_ref,
    row_ref,
    edge_ref,
    grads_ref,
):
    frame = pl.program_id(0)
    rem = max(width + 4 - LANES, 0)
    chunks = -(-width // LANES)

    @pl.when(frame == 0)
    def _():
        taps_ref[...] = jnp.zeros_like(taps_ref)
        for s in range(3):
            zero_row = jnp.zeros(grads_ref.shape[2:], grads_ref.dtype)
            grads_ref[s, 0] = zero_row
            grads_ref[s, height + 1] = zero_row

    is_near = code_ref[frame] % 2 != 0
    message = jnp.where(is_near, near_ref[0].astype(jnp.float32), far_ref[0].astype(jnp.float32))
    mains = [message[k * height : (k + 1) * height] for k in range(3)]
    if rem > 0:
        tail = message[3 * height : 4 * height]
    for k in range(3):
        if rem > 0:
            line = jnp.concatenate([mains[k], tail[:, k * rem : (k + 1) * rem]], axis=1)
        else:
            line = mains[k]
        for s in range(3):
            for c in range(chunks):
                start = 3 - s + c * LANES
                stop = min(start + LANES, width + 4)
                part = line[:, start:stop]
                if stop - start < LANES:
                    blank = jnp.zeros((height, LANES - (stop - start)), jnp.float32)
                    part = jnp.concatenate([part, blank], axis=1)
                taps_ref[c, pl.ds(SUB + 3 * s + k, height, stride=SUB), :] = part
    pieces = mains + ([tail] if rem > 0 else [])
    wide = jnp.concatenate(pieces, axis=1).astype(jnp.bfloat16)
    per_tap = jnp.dot(wide, w_edge_ref[...], preferred_element_type=jnp.float32)
    zeros = jnp.zeros((1, 2 * LANES), jnp.float32)
    first, middle, last = (per_tap[:, i * 2 * LANES : (i + 1) * 2 * LANES] for i in range(3))
    edge = (
        jnp.concatenate([first[1:], zeros], axis=0)
        + middle
        + jnp.concatenate([zeros, last[: height - 1]], axis=0)
    )
    tile = lax.axis_index("tile")
    has_left = jnp.where(tile > 0, 1.0, 0.0)
    has_right = jnp.where(tile < lax.axis_size("tile") - 1, 1.0, 0.0)
    left_slope = silu_slope(left_ref[0].astype(jnp.float32)) * has_left
    right_slope = silu_slope(right_ref[0].astype(jnp.float32)) * has_right
    edge_ref[:, :LANES] = edge[:, :LANES] * left_slope
    edge_ref[:, LANES:] = edge[:, LANES:] * right_slope

    pairs = block_rows // 2

    def produce(block):
        base = block * block_rows
        lhs = jnp.concatenate(
            [
                taps_ref[c, (base + 2 * p) * SUB : (base + 2 * p + 4) * SUB, :]
                .T[: min(LANES, width - c * LANES)]
                .astype(jnp.bfloat16)
                for p in range(pairs)
                for c in range(chunks)
            ],
            axis=0,
        )
        back = jnp.dot(lhs, w_one_ref[...], preferred_element_type=jnp.float32)
        for i in range(block_rows):
            y = base + i
            p, h = i // 2, i % 2
            part = back[p * width : (p + 1) * width, h * LANES : (h + 1) * LANES]
            value = part * silu_slope(act_ref[0, y].astype(jnp.float32))
            slot = i % 4
            row_ref[slot, 8 : 8 + width, :] = value
            row_ref[slot, 7:8, :] = edge_ref[y : y + 1, :LANES]
            row_ref[slot, 8 + width : 9 + width, :] = edge_ref[y : y + 1, LANES:]
            grads_ref[0, y + 1] = row_ref[slot, 9 : 9 + width, :].astype(jnp.bfloat16)
            grads_ref[1, y + 1] = value.astype(jnp.bfloat16)
            grads_ref[2, y + 1] = row_ref[slot, 7 : 7 + width, :].astype(jnp.bfloat16)

    def consume(block):
        base = block * block_rows
        slabs = []
        for j in range(4):
            for s in range(3):
                slabs.append(
                    jnp.concatenate([grads_ref[s, base + 2 * p + j] for p in range(pairs)], axis=0)
                )
        lhs = jnp.concatenate(slabs, axis=1)
        half = lhs.shape[1] // 2
        total = jnp.dot(lhs[:, :half], w_two_ref[:half], preferred_element_type=jnp.float32)
        total += jnp.dot(lhs[:, half:], w_two_ref[half:], preferred_element_type=jnp.float32)
        for i in range(block_rows):
            p, h = i // 2, i % 2
            part = total[p * width : (p + 1) * width, h * LANES : (h + 1) * LANES]
            centre = grads_ref[1, base + i + 1].astype(jnp.float32)
            out_ref[0, base + i] = (part + centre).astype(out_ref.dtype)

    blocks = height // block_rows
    produce(0)
    for block in range(blocks):
        if block + 1 < blocks:
            produce(block + 1)
        consume(block)


def decoder_weights(conv_out_weight, conv_weight, height, width):
    rem = max(width + 4 - LANES, 0)
    taps_out = 0.5 * conv_out_weight.transpose(0, 1, 3, 2)
    channels = conv_weight.shape[2]
    small = jnp.pad(
        taps_out.reshape(3, 9, channels), ((0, 0), (0, SUB - 9), (0, 0))
    )
    none = jnp.zeros_like(small[0])
    w_one = jnp.concatenate(
        [
            jnp.stack([small[h - j + 2] if 0 <= h - j + 2 < 3 else none for j in range(4)])
            for h in range(2)
        ],
        axis=2,
    ).reshape(4 * SUB, 2 * channels)
    big = conv_weight.transpose(0, 1, 3, 2)
    none = jnp.zeros_like(big[0])
    w_two = jnp.concatenate(
        [
            jnp.stack([big[h - j + 2] if 0 <= h - j + 2 < 3 else none for j in range(4)])
            for h in range(2)
        ],
        axis=3,
    ).reshape(4 * 3 * channels, 2 * channels)
    flipped = taps_out[:, ::-1].transpose(0, 2, 1, 3)
    groups = 4 if rem > 0 else 3
    sides = []
    for r in range(3):
        left = jnp.zeros((groups * LANES, channels), conv_out_weight.dtype)
        right = jnp.zeros((groups * LANES, channels), conv_out_weight.dtype)
        for k in range(3):
            left = left.at[k * LANES : k * LANES + 3].set(flipped[r, k])
            for i in range(3):
                lane = width + 1 + i
                if lane < LANES:
                    place = k * LANES + lane
                else:
                    place = 3 * LANES + k * rem + lane - LANES
                right = right.at[place].set(flipped[r, k, i])
        sides.extend([left, right])
    w_edge = jnp.concatenate(sides, axis=1)
    return w_edge, w_one, w_two


def decode(code, near, far, left, right, activations, weights, block_rows):
    frames, height, width, channels = activations.shape
    rows = near.shape[1]
    w_edge, w_one, w_two = weights
    whole = lambda shape: pl.BlockSpec(shape, lambda f, *_: (0,) * len(shape))
    padded = -(-(width + 9) // 8) * 8 + 8
    return pl.pallas_call(
        functools.partial(decoder_kernel, height, width, block_rows),
        out_shape=jax.ShapeDtypeStruct(activations.shape, jnp.bfloat16),
        grid_spec=pltpu.PrefetchScalarGridSpec(
            num_scalar_prefetch=1,
            grid=(frames,),
            in_specs=[
                pl.BlockSpec((1, rows, LANES), lambda f, code: (code[f] // 2, 0, 0)),
                pl.BlockSpec((1, rows, LANES), lambda f, code: (f, 0, 0)),
                pl.BlockSpec((1, height, channels), lambda f, *_: (f, 0, 0)),
                pl.BlockSpec((1, height, channels), lambda f, *_: (f, 0, 0)),
                pl.BlockSpec((1, height, width, channels), lambda f, *_: (f, 0, 0, 0)),
                whole(w_edge.shape),
                whole(w_one.shape),
                whole(w_two.shape),
            ],
            out_specs=pl.BlockSpec((1, height, width, channels), lambda f, *_: (f, 0, 0, 0)),
            scratch_shapes=[
                pltpu.VMEM((-(-width // LANES), (height + 2) * SUB, LANES), jnp.float32),
                pltpu.VMEM((4, padded, channels), jnp.float32),
                pltpu.VMEM((height, 2 * channels), jnp.float32),
                pltpu.VMEM((3, height + 2, width, channels), jnp.bfloat16),
            ],
        ),
        compiler_params=pltpu.CompilerParams(vmem_limit_bytes=56 * 1024 * 1024),
        cost_estimate=pl.CostEstimate(
            flops=2 * frames * height * width * channels * (12 * channels + 64),
            bytes_accessed=4 * frames * height * width * channels,
            transcendentals=frames * height * width * channels,
        ),
    )(code, near, far, left, right, activations, w_edge, w_one, w_two)


def dot(left, right, dims=((1,), (0,))):
    return lax.dot_general(left, right, (dims, ((), ())), preferred_element_type=WIDE)


def dot_rows(left, right):
    return dot(left, right, ((1,), (1,)))


def tower_kernel(
    tiles,
    pixel_ref,
    patch_raw_ref,
    gain_ref,
    qkv_ref,
    proj_ref,
    post_gain_ref,
    text_ref,
    strip_ref,
    order_ref,
    patches_ref,
    unit_ref,
    scale_ref,
    normed_ref,
    heads_ref,
    head_scale_ref,
    probs_ref,
    column_ref,
    slope_ref,
    back_ref,
    grad_ref,
    tangent_ref,
    qkv_copy_ref,
    proj_copy_ref,
    patch_order_ref,
    sems,
):
    qkv_copy = pltpu.make_async_copy(qkv_ref, qkv_copy_ref, sems.at[0])
    proj_copy = pltpu.make_async_copy(proj_ref, proj_copy_ref, sems.at[1])
    qkv_copy.start()
    proj_copy.start()
    slots, colour_rows, columns = pixel_ref.shape
    height = colour_rows // 3
    dim = gain_ref.shape[1]
    across = columns // PATCH
    down = height // PATCH
    tokens = across * down
    bands = slots * down
    total = slots * tokens
    width = columns // tiles
    rem = max(width + 4 - LANES, 0)
    block = 2 * LANES

    column_id = lax.broadcasted_iota(jnp.int32, (columns, 1), 0)
    goal = (column_id % PATCH) * LANES + column_id // PATCH
    for j in range(PATCH):
        lane_id = lax.broadcasted_iota(jnp.int32, (columns, LANES), 1) + j * LANES
        order_ref[:, j * LANES : (j + 1) * LANES] = jnp.where(goal == lane_id, 1.0, 0.0).astype(
            NARROW
        )

    entries_count = patch_raw_ref.shape[0]
    row_id = lax.broadcasted_iota(jnp.int32, (entries_count, 1), 0)
    lines_count = entries_count // PATCH
    goal = (row_id % lines_count) * PATCH + row_id // lines_count
    entry_id = lax.broadcasted_iota(jnp.int32, (entries_count, entries_count), 1)
    move = jnp.where(goal == entry_id, 1.0, 0.0).astype(NARROW)
    patch_ref = patch_order_ref
    for n in range(dim // block):
        at = slice(n * block, (n + 1) * block)
        patch_ref[:, at] = dot(move, patch_raw_ref[:, at]).astype(NARROW)

    every = dot(
        jnp.concatenate([pixel_ref[f] for f in range(slots)], axis=0), order_ref[...]
    )
    for f in range(slots):
        spread = every[f * colour_rows : (f + 1) * colour_rows]
        for py in range(down):
            entries = jnp.concatenate(
                [
                    spread[
                        k * height + py * PATCH : k * height + (py + 1) * PATCH,
                        j * LANES : (j + 1) * LANES,
                    ]
                    for j in range(PATCH)
                    for k in range(3)
                ],
                axis=0,
            )
            start = (f * down + py) * across
            patches_ref[start : start + across, :] = entries.T[:across].astype(NARROW)

    @pl.loop(0, dim // block, unroll=2)
    def _(n):
        at = pl.ds(pl.multiple_of(n * block, block), block)
        unit_ref[:, at] = dot(patches_ref[...], patch_ref[:, at])

    means = [jnp.zeros((1, dim), WIDE) for _ in range(slots)]
    for b in range(bands):
        rows = slice(b * across, (b + 1) * across)
        embedded = unit_ref[rows, :]
        means[b // down] += jnp.sum(embedded, axis=0, keepdims=True)
        centred = embedded - jnp.mean(embedded, axis=1, keepdims=True)
        scale = lax.rsqrt(jnp.mean(centred * centred, axis=1, keepdims=True) + EPS)
        unit = centred * scale
        unit_ref[rows, :] = unit
        scale_ref[rows, :] = jnp.broadcast_to(scale, (across, LANES))
        normed_ref[rows, :] = (unit * gain_ref[...]).astype(NARROW)
    means = [value * (1.0 / tokens) for value in means]

    qkv_copy.wait()
    proj_copy.wait()
    qkv_ref, proj_ref = qkv_copy_ref, proj_copy_ref

    row_head = lax.broadcasted_iota(jnp.int32, (block, block), 0) // HEAD_DIM
    lane_head = lax.broadcasted_iota(jnp.int32, (block, block), 1) // HEAD_DIM
    average = jnp.where(row_head == lane_head, 1.0 / HEAD_DIM, 0.0).astype(NARROW)

    @pl.loop(0, 2 * dim // block)
    def _(n):
        at = pl.multiple_of(n * block, block)
        both = dot(normed_ref[...], qkv_ref[:, pl.ds(at, block)])
        centred = both - dot(both.astype(NARROW), average)
        scale = lax.rsqrt(dot((centred * centred).astype(NARROW), average) + EPS)
        head_scale_ref[:, pl.ds(at, block)] = scale
        heads_ref[:, pl.ds(at, block)] = (centred * scale).astype(NARROW)

    lane = lax.broadcasted_iota(jnp.int32, (1, LANES), 1)
    sides = [lane < HEAD_DIM, lane >= HEAD_DIM]
    factor = 1.0 / HEAD_DIM**0.5
    pairs = dim // LANES

    def pair_at(index):
        f = index // pairs
        i = index % pairs
        rows = pl.ds(pl.multiple_of(f * tokens, SUB), tokens)
        query_at = pl.ds(pl.multiple_of(i * LANES, LANES), LANES)
        key_at = pl.ds(pl.multiple_of(dim + i * LANES, LANES), LANES)
        return rows, query_at, key_at

    @pl.loop(0, slots * pairs, unroll=8)
    def _(index):
        rows, query_at, key_at = pair_at(index)
        query = heads_ref[rows, query_at]
        key = heads_ref[rows, key_at]
        masks = [jnp.where(side, factor, 0.0).astype(NARROW) for side in sides]
        both = dot_rows(jnp.concatenate([query * mask for mask in masks], axis=0), key)
        for side in range(2):
            exps = jnp.exp(both[side * tokens : (side + 1) * tokens])
            probs = exps * (1.0 / jnp.sum(exps, axis=1, keepdims=True))
            column_ref[pl.ds(2 * index + side, 1), :] = jnp.sum(probs, axis=0, keepdims=True)
            probs_ref[2 * index + side] = probs.astype(NARROW)

    value_weight = qkv_ref.at[:, 2 * dim : 3 * dim]
    head_row = lax.broadcasted_iota(jnp.int32, (HEADS, dim), 0)
    head_lane = lax.broadcasted_iota(jnp.int32, (HEADS, dim), 1) // HEAD_DIM
    own_head = head_row == head_lane
    normed = [normed_ref[f * tokens : (f + 1) * tokens, :] for f in range(slots)]
    weights = [column_ref[f * HEADS : (f + 1) * HEADS, :].astype(NARROW) for f in range(slots)]
    mixed = jnp.concatenate([dot(weights[f], normed[f]) for f in range(slots)], axis=0)
    values = dot(mixed.astype(NARROW), value_weight[...])
    context = jnp.concatenate(
        [
            jnp.broadcast_to(
                jnp.sum(
                    jnp.where(own_head, values[f * HEADS : (f + 1) * HEADS], 0.0),
                    axis=0,
                    keepdims=True,
                )
                * (1.0 / tokens),
                (8, dim),
            )
            for f in range(slots)
        ],
        axis=0,
    )
    mean_rows = jnp.concatenate([jnp.broadcast_to(m, (8, dim)) for m in means], axis=0)
    pooled = mean_rows + dot(context.astype(NARROW), proj_ref[...])
    centred = pooled - jnp.mean(pooled, axis=1, keepdims=True)
    scale = lax.rsqrt(jnp.mean(centred * centred, axis=1, keepdims=True) + EPS)
    unit = centred * scale
    post = unit * post_gain_ref[...]
    text = text_ref[...]
    text = text * lax.rsqrt(jnp.sum(text * text, axis=1, keepdims=True) + EPS)
    along = jnp.sum(post * text, axis=1, keepdims=True)
    length = lax.rsqrt(jnp.sum(post * post, axis=1, keepdims=True) + EPS)
    post_back = (LOSS_SCALE * LOGIT_SCALE) * (length * text - along * length**3 * post)
    unit_back = post_back * post_gain_ref[...]
    pooled_back = scale * (
        unit_back
        - jnp.mean(unit_back, axis=1, keepdims=True)
        - unit * jnp.mean(unit_back * unit, axis=1, keepdims=True)
    )
    token_back = pooled_back * (1.0 / tokens)
    context_back = dot_rows(token_back.astype(NARROW), proj_ref[...])
    by_head = jnp.concatenate(
        [
            jnp.where(own_head, jnp.broadcast_to(context_back[8 * f : 8 * f + 1], (HEADS, dim)), 0.0)
            for f in range(slots)
        ],
        axis=0,
    )
    value_back = dot_rows(by_head.astype(NARROW), value_weight[...]).astype(NARROW)
    for f in range(slots):
        slope_ref[f * HEADS : (f + 1) * HEADS, :] = dot_rows(
            value_back[f * HEADS : (f + 1) * HEADS], normed[f]
        )

    @pl.loop(0, slots * pairs, unroll=8)
    def _(index):
        rows, query_at, key_at = pair_at(index)
        query = heads_ref[rows, query_at]
        key = heads_ref[rows, key_at]
        scores_back = []
        for side in range(2):
            probs = probs_ref[2 * index + side].astype(WIDE)
            slope = slope_ref[pl.ds(2 * index + side, 1), :]
            middle = jnp.sum(probs * slope, axis=1, keepdims=True)
            scores_back.append((probs * (slope - middle)).astype(NARROW))
        query_back = dot(jnp.concatenate(scores_back, axis=0), key)
        key_back = jnp.concatenate(
            [dot(part, query, ((0,), (0,))) for part in scores_back], axis=0
        )
        gradient = jnp.concatenate(
            [
                jnp.where(sides[0], query_back[:tokens], query_back[tokens:]),
                jnp.where(sides[0], key_back[:tokens], key_back[tokens:]),
            ],
            axis=1,
        )
        unit = jnp.concatenate([query, key], axis=1).astype(WIDE)
        plain = dot(gradient.astype(NARROW), average)
        along = dot((gradient * unit).astype(NARROW), average)
        value = factor * (gradient - plain - unit * along)
        back_ref[rows, query_at] = (head_scale_ref[rows, query_at] * value[:, :LANES]).astype(NARROW)
        back_ref[rows, key_at] = (head_scale_ref[rows, key_at] * value[:, LANES:]).astype(NARROW)

    for f in range(slots):
        grad_ref[f * tokens : (f + 1) * tokens, :] = dot(
            weights[f], value_back[f * HEADS : (f + 1) * HEADS], ((0,), (0,))
        )

    @pl.loop(0, dim // block, unroll=2)
    def _(n):
        at = pl.ds(pl.multiple_of(n * block, block), block)
        grad_ref[:, at] += dot_rows(back_ref[...], qkv_ref[at, : 2 * dim])

    tangent_ref[...] = jnp.zeros_like(tangent_ref)
    for b in range(bands):
        rows = slice(b * across, (b + 1) * across)
        f = b // down
        unit = unit_ref[rows, :]
        unit_back = grad_ref[rows, :] * gain_ref[...]
        value = (
            unit_back
            - jnp.mean(unit_back, axis=1, keepdims=True)
            - unit * jnp.mean(unit_back * unit, axis=1, keepdims=True)
        )
        value = scale_ref[rows, :1] * value + token_back[8 * f : 8 * f + 1]
        tangent_ref[b * LANES : b * LANES + across, :] = value.astype(NARROW)

    lines = []
    for f in range(slots):
        entries = dot_rows(
            patch_ref[...], tangent_ref[f * down * LANES : (f + 1) * down * LANES, :]
        ).astype(NARROW)
        for k in range(3):
            for py in range(down):
                lines.append(
                    jnp.concatenate(
                        [
                            entries[
                                (3 * j + k) * PATCH : (3 * j + k + 1) * PATCH,
                                py * LANES : (py + 1) * LANES,
                            ]
                            for j in range(PATCH)
                        ],
                        axis=1,
                    )
                )
    every = dot_rows(jnp.concatenate(lines, axis=0), order_ref[...])
    for f in range(slots):
        frame = every[f * colour_rows : (f + 1) * colour_rows]
        frame = jnp.concatenate(
            [
                jnp.zeros((colour_rows, 2), WIDE),
                frame,
                jnp.zeros((colour_rows, LANES - 2), WIDE),
            ],
            axis=1,
        )
        for t in range(tiles):
            base = t * width
            main = frame[:, base : base + LANES]
            if rem == 0 and width + 4 < LANES:
                main = jnp.where(lane < width + 4, main, 0.0)
            strip_ref[t, f, :colour_rows, :] = main.astype(NARROW)
            if rem > 0:
                tail = [
                    frame[
                        k * height : (k + 1) * height, base + LANES : base + LANES + rem
                    ]
                    for k in range(3)
                ]
                tail.append(jnp.zeros((height, LANES - 3 * rem), WIDE))
                strip_ref[t, f, colour_rows:, :] = jnp.concatenate(tail, axis=1).astype(NARROW)


def tower(
    pixels, patch_weight, norm_gain, qkv_weight, out_weight, post_gain, text_embed, tiles
):
    slots, colours, height, columns = pixels.shape
    dim = norm_gain.shape[0]
    across = columns // PATCH
    down = height // PATCH
    tokens = across * down
    total = slots * tokens
    width = columns // tiles
    rows = colours * height + (height if width + 4 > LANES else 0)
    entries = colours * PATCH * PATCH
    vmem = pl.BlockSpec(memory_space=pltpu.VMEM)
    return pl.pallas_call(
        functools.partial(tower_kernel, tiles),
        out_shape=jax.ShapeDtypeStruct((tiles, slots, rows, LANES), NARROW),
        in_specs=[vmem] * 3 + [pl.BlockSpec(memory_space=pl.ANY)] * 2 + [vmem] * 2,
        out_specs=vmem,
        scratch_shapes=[
            pltpu.VMEM((columns, PATCH * LANES), NARROW),
            pltpu.VMEM((total, entries), NARROW),
            pltpu.VMEM((total, dim), WIDE),
            pltpu.VMEM((total, LANES), WIDE),
            pltpu.VMEM((total, dim), NARROW),
            pltpu.VMEM((total, 2 * dim), NARROW),
            pltpu.VMEM((total, 2 * dim), WIDE),
            pltpu.VMEM((slots * HEADS, tokens, tokens), NARROW),
            pltpu.VMEM((slots * HEADS, tokens), WIDE),
            pltpu.VMEM((slots * HEADS, tokens), WIDE),
            pltpu.VMEM((total, 2 * dim), NARROW),
            pltpu.VMEM((total, dim), WIDE),
            pltpu.VMEM((slots * down * LANES, dim), NARROW),
            pltpu.VMEM(qkv_weight.shape, NARROW),
            pltpu.VMEM(out_weight.shape, NARROW),
            pltpu.VMEM((entries, dim), NARROW),
            pltpu.SemaphoreType.DMA((2,)),
        ],
        compiler_params=pltpu.CompilerParams(vmem_limit_bytes=60 * 1024 * 1024),
        cost_estimate=pl.CostEstimate(
            flops=2 * total * dim * (2 * entries + 4 * dim + 4 * tokens),
            bytes_accessed=2 * (entries * dim + 4 * dim * dim),
            transcendentals=slots * HEADS * tokens * tokens,
        ),
    )(
        pixels.reshape(slots, colours * height, columns),
        patch_weight,
        norm_gain[None],
        qkv_weight,
        out_weight,
        post_gain[None],
        text_embed[None],
    )


def frame_rank(owner):
    frame_ids = jnp.arange(owner.shape[0], dtype=jnp.int32)
    same_owner = owner[:, None] == owner[None, :]
    earlier = frame_ids[None, :] < frame_ids[:, None]
    return jnp.sum((same_owner & earlier).astype(jnp.int32), axis=1)


def local(
    pixels,
    owner,
    patch_weight,
    norm_gain,
    qkv_weight,
    out_weight,
    post_gain,
    text_embed,
    conv_out_weight,
    conv_weight,
    activations,
):
    tile_count = lax.axis_size("tile")
    core_count = lax.axis_size("tm")
    core = lax.axis_index("tm")
    frames, height, width, channels = activations.shape
    slots = pixels.shape[0]
    ranks_all = frame_rank(owner)

    outgoing = tower(
        pixels, patch_weight, norm_gain, qkv_weight, out_weight, post_gain, text_embed, tile_count
    )
    outgoing, origin = lax.optimization_barrier((outgoing, jnp.int32(0)))
    rows = outgoing.shape[2]
    near = lax.all_to_all(outgoing, "tile", split_axis=0, concat_axis=0, tiled=True)
    up = [(i, i + 1) for i in range(tile_count - 1)]
    down = [(j, i) for i, j in up]
    left = lax.ppermute(lax.dynamic_index_in_dim(activations, origin + (width - 1), 2, False), "tile", up)
    right = lax.ppermute(lax.dynamic_index_in_dim(activations, origin, 2, False), "tile", down)

    near = near.reshape(tile_count * slots, rows, LANES)
    pick_all = (owner // core_count) * slots + ranks_all
    code_all = 2 * pick_all + (owner % core_count == core).astype(jnp.int32)
    by_core = lambda values, index: lax.dynamic_slice_in_dim(values, index * frames, frames)
    code = by_core(code_all, core)
    weights = decoder_weights(conv_out_weight, conv_weight, height, width)
    near, code, left, right, *weights = lax.optimization_barrier(
        (near, code, left, right, *weights)
    )
    other = 1 - core
    far = lax.ppermute(jnp.take(near, by_core(pick_all, other), axis=0), "tm", [(0, 1), (1, 0)])
    return decode(
        code,
        near,
        far,
        left,
        right,
        activations,
        weights,
        4,
    )


def solution(mesh):
    placed = (
        P(("groups", "tile", "tm"), None, None, None),
        P("groups"),
        P(),
        P(),
        P(),
        P(),
        P(),
        P("groups"),
        P(),
        P(),
        P(("groups", "tm"), None, "tile", None),
    )
    return jax.shard_map(
        local,
        mesh=mesh,
        in_specs=placed,
        out_specs=P(("groups", "tm"), None, "tile", None),
        check_vma=False,
    )
```

```python
import functools

import jax
import jax.numpy as jnp
from jax import lax
from jax.experimental import pallas as pl
from jax.experimental.pallas import tpu as pltpu
from jax.sharding import PartitionSpec as P

HEADS = 16
HEAD_DIM = 64
PATCH = 16
EPS = 1e-06
LOGIT_SCALE = 100.0
LOSS_SCALE = 64.0

LANES = 128
SUB = 16
NARROW = jnp.bfloat16
WIDE = jnp.float32


def silu_slope(pre_value):
    half = 0.5 * pre_value
    gate = jnp.tanh(half)
    return (1.0 + gate) * (1.0 + half * (1.0 - gate))


def decoder_kernel(
    height,
    width,
    block_rows,
    code_ref,
    near_ref,
    far_ref,
    left_ref,
    right_ref,
    act_ref,
    w_edge_ref,
    w_one_ref,
    w_two_ref,
    out_ref,
    taps_ref,
    row_ref,
    edge_ref,
    grads_ref,
):
    frame = pl.program_id(0)
    rem = max(width + 4 - LANES, 0)
    chunks = -(-width // LANES)

    @pl.when(frame == 0)
    def _():
        taps_ref[...] = jnp.zeros_like(taps_ref)
        for s in range(3):
            zero_row = jnp.zeros(grads_ref.shape[2:], grads_ref.dtype)
            grads_ref[s, 0] = zero_row
            grads_ref[s, height + 1] = zero_row

    is_near = code_ref[frame] % 2 != 0
    message = jnp.where(is_near, near_ref[0].astype(jnp.float32), far_ref[0].astype(jnp.float32))
    mains = [message[k * height : (k + 1) * height] for k in range(3)]
    if rem > 0:
        tail = message[3 * height : 4 * height]
    for k in range(3):
        if rem > 0:
            line = jnp.concatenate([mains[k], tail[:, k * rem : (k + 1) * rem]], axis=1)
        else:
            line = mains[k]
        for s in range(3):
            for c in range(chunks):
                start = 3 - s + c * LANES
                stop = min(start + LANES, width + 4)
                part = line[:, start:stop]
                if stop - start < LANES:
                    blank = jnp.zeros((height, LANES - (stop - start)), jnp.float32)
                    part = jnp.concatenate([part, blank], axis=1)
                taps_ref[c, pl.ds(SUB + 3 * s + k, height, stride=SUB), :] = part
    pieces = mains + ([tail] if rem > 0 else [])
    wide = jnp.concatenate(pieces, axis=1).astype(jnp.bfloat16)
    per_tap = jnp.dot(wide, w_edge_ref[...], preferred_element_type=jnp.float32)
    zeros = jnp.zeros((1, 2 * LANES), jnp.float32)
    first, middle, last = (per_tap[:, i * 2 * LANES : (i + 1) * 2 * LANES] for i in range(3))
    edge = (
        jnp.concatenate([first[1:], zeros], axis=0)
        + middle
        + jnp.concatenate([zeros, last[: height - 1]], axis=0)
    )
    tile = lax.axis_index("tile")
    has_left = jnp.where(tile > 0, 1.0, 0.0)
    has_right = jnp.where(tile < lax.axis_size("tile") - 1, 1.0, 0.0)
    left_slope = silu_slope(left_ref[0].astype(jnp.float32)) * has_left
    right_slope = silu_slope(right_ref[0].astype(jnp.float32)) * has_right
    edge_ref[:, :LANES] = edge[:, :LANES] * left_slope
    edge_ref[:, LANES:] = edge[:, LANES:] * right_slope

    pairs = block_rows // 2

    def produce(block):
        base = block * block_rows
        lhs = jnp.concatenate(
            [
                taps_ref[c, (base + 2 * p) * SUB : (base + 2 * p + 4) * SUB, :]
                .T[: min(LANES, width - c * LANES)]
                .astype(jnp.bfloat16)
                for p in range(pairs)
                for c in range(chunks)
            ],
            axis=0,
        )
        back = jnp.dot(lhs, w_one_ref[...], preferred_element_type=jnp.float32)
        for i in range(block_rows):
            y = base + i
            p, h = i // 2, i % 2
            part = back[p * width : (p + 1) * width, h * LANES : (h + 1) * LANES]
            value = part * silu_slope(act_ref[0, y].astype(jnp.float32))
            slot = i % 4
            row_ref[slot, 8 : 8 + width, :] = value
            row_ref[slot, 7:8, :] = edge_ref[y : y + 1, :LANES]
            row_ref[slot, 8 + width : 9 + width, :] = edge_ref[y : y + 1, LANES:]
            grads_ref[0, y + 1] = row_ref[slot, 9 : 9 + width, :].astype(jnp.bfloat16)
            grads_ref[1, y + 1] = value.astype(jnp.bfloat16)
            grads_ref[2, y + 1] = row_ref[slot, 7 : 7 + width, :].astype(jnp.bfloat16)

    def consume(block):
        base = block * block_rows
        slabs = []
        for j in range(4):
            for s in range(3):
                slabs.append(
                    jnp.concatenate([grads_ref[s, base + 2 * p + j] for p in range(pairs)], axis=0)
                )
        lhs = jnp.concatenate(slabs, axis=1)
        half = lhs.shape[1] // 2
        total = jnp.dot(lhs[:, :half], w_two_ref[:half], preferred_element_type=jnp.float32)
        total += jnp.dot(lhs[:, half:], w_two_ref[half:], preferred_element_type=jnp.float32)
        for i in range(block_rows):
            p, h = i // 2, i % 2
            part = total[p * width : (p + 1) * width, h * LANES : (h + 1) * LANES]
            centre = grads_ref[1, base + i + 1].astype(jnp.float32)
            out_ref[0, base + i] = (part + centre).astype(out_ref.dtype)

    blocks = height // block_rows
    produce(0)
    for block in range(blocks):
        if block + 1 < blocks:
            produce(block + 1)
        consume(block)


def decoder_weights(conv_out_weight, conv_weight, height, width):
    rem = max(width + 4 - LANES, 0)
    taps_out = 0.5 * conv_out_weight.transpose(0, 1, 3, 2)
    channels = conv_weight.shape[2]
    small = jnp.pad(
        taps_out.reshape(3, 9, channels), ((0, 0), (0, SUB - 9), (0, 0))
    )
    none = jnp.zeros_like(small[0])
    w_one = jnp.concatenate(
        [
            jnp.stack([small[h - j + 2] if 0 <= h - j + 2 < 3 else none for j in range(4)])
            for h in range(2)
        ],
        axis=2,
    ).reshape(4 * SUB, 2 * channels)
    big = conv_weight.transpose(0, 1, 3, 2)
    none = jnp.zeros_like(big[0])
    w_two = jnp.concatenate(
        [
            jnp.stack([big[h - j + 2] if 0 <= h - j + 2 < 3 else none for j in range(4)])
            for h in range(2)
        ],
        axis=3,
    ).reshape(4 * 3 * channels, 2 * channels)
    flipped = taps_out[:, ::-1].transpose(0, 2, 1, 3)
    groups = 4 if rem > 0 else 3
    sides = []
    for r in range(3):
        left = jnp.zeros((groups * LANES, channels), conv_out_weight.dtype)
        right = jnp.zeros((groups * LANES, channels), conv_out_weight.dtype)
        for k in range(3):
            left = left.at[k * LANES : k * LANES + 3].set(flipped[r, k])
            for i in range(3):
                lane = width + 1 + i
                if lane < LANES:
                    place = k * LANES + lane
                else:
                    place = 3 * LANES + k * rem + lane - LANES
                right = right.at[place].set(flipped[r, k, i])
        sides.extend([left, right])
    w_edge = jnp.concatenate(sides, axis=1)
    return w_edge, w_one, w_two


def decode(code, near, far, left, right, activations, weights, block_rows):
    frames, height, width, channels = activations.shape
    rows = near.shape[1]
    w_edge, w_one, w_two = weights
    whole = lambda shape: pl.BlockSpec(shape, lambda f, *_: (0,) * len(shape))
    padded = -(-(width + 9) // 8) * 8 + 8
    return pl.pallas_call(
        functools.partial(decoder_kernel, height, width, block_rows),
        out_shape=jax.ShapeDtypeStruct(activations.shape, jnp.bfloat16),
        grid_spec=pltpu.PrefetchScalarGridSpec(
            num_scalar_prefetch=1,
            grid=(frames,),
            in_specs=[
                pl.BlockSpec((1, rows, LANES), lambda f, code: (code[f] // 2, 0, 0)),
                pl.BlockSpec((1, rows, LANES), lambda f, code: (f, 0, 0)),
                pl.BlockSpec((1, height, channels), lambda f, *_: (f, 0, 0)),
                pl.BlockSpec((1, height, channels), lambda f, *_: (f, 0, 0)),
                pl.BlockSpec((1, height, width, channels), lambda f, *_: (f, 0, 0, 0)),
                whole(w_edge.shape),
                whole(w_one.shape),
                whole(w_two.shape),
            ],
            out_specs=pl.BlockSpec((1, height, width, channels), lambda f, *_: (f, 0, 0, 0)),
            scratch_shapes=[
                pltpu.VMEM((-(-width // LANES), (height + 2) * SUB, LANES), jnp.float32),
                pltpu.VMEM((4, padded, channels), jnp.float32),
                pltpu.VMEM((height, 2 * channels), jnp.float32),
                pltpu.VMEM((3, height + 2, width, channels), jnp.bfloat16),
            ],
        ),
        compiler_params=pltpu.CompilerParams(vmem_limit_bytes=56 * 1024 * 1024),
        cost_estimate=pl.CostEstimate(
            flops=2 * frames * height * width * channels * (12 * channels + 64),
            bytes_accessed=4 * frames * height * width * channels,
            transcendentals=frames * height * width * channels,
        ),
    )(code, near, far, left, right, activations, w_edge, w_one, w_two)


def dot(left, right, dims=((1,), (0,))):
    return lax.dot_general(left, right, (dims, ((), ())), preferred_element_type=WIDE)


def dot_rows(left, right):
    return dot(left, right, ((1,), (1,)))


def tower_kernel(
    tiles,
    pixel_ref,
    patch_raw_ref,
    gain_ref,
    qkv_ref,
    proj_ref,
    post_gain_ref,
    text_ref,
    strip_ref,
    order_ref,
    patches_ref,
    unit_ref,
    scale_ref,
    normed_ref,
    heads_ref,
    head_scale_ref,
    probs_ref,
    column_ref,
    slope_ref,
    back_ref,
    grad_ref,
    tangent_ref,
    qkv_copy_ref,
    proj_copy_ref,
    patch_order_ref,
    sems,
):
    qkv_copy = pltpu.make_async_copy(qkv_ref, qkv_copy_ref, sems.at[0])
    proj_copy = pltpu.make_async_copy(proj_ref, proj_copy_ref, sems.at[1])
    qkv_copy.start()
    proj_copy.start()
    slots, colour_rows, columns = pixel_ref.shape
    height = colour_rows // 3
    dim = gain_ref.shape[1]
    across = columns // PATCH
    down = height // PATCH
    tokens = across * down
    bands = slots * down
    total = slots * tokens
    width = columns // tiles
    rem = max(width + 4 - LANES, 0)
    block = 2 * LANES

    column_id = lax.broadcasted_iota(jnp.int32, (columns, 1), 0)
    goal = (column_id % PATCH) * LANES + column_id // PATCH
    for j in range(PATCH):
        lane_id = lax.broadcasted_iota(jnp.int32, (columns, LANES), 1) + j * LANES
        order_ref[:, j * LANES : (j + 1) * LANES] = jnp.where(goal == lane_id, 1.0, 0.0).astype(
            NARROW
        )

    entries_count = patch_raw_ref.shape[0]
    row_id = lax.broadcasted_iota(jnp.int32, (entries_count, 1), 0)
    lines_count = entries_count // PATCH
    goal = (row_id % lines_count) * PATCH + row_id // lines_count
    entry_id = lax.broadcasted_iota(jnp.int32, (entries_count, entries_count), 1)
    move = jnp.where(goal == entry_id, 1.0, 0.0).astype(NARROW)
    patch_ref = patch_order_ref
    for n in range(dim // block):
        at = slice(n * block, (n + 1) * block)
        patch_ref[:, at] = dot(move, patch_raw_ref[:, at]).astype(NARROW)

    every = dot(
        jnp.concatenate([pixel_ref[f] for f in range(slots)], axis=0), order_ref[...]
    )
    for f in range(slots):
        spread = every[f * colour_rows : (f + 1) * colour_rows]
        for py in range(down):
            entries = jnp.concatenate(
                [
                    spread[
                        k * height + py * PATCH : k * height + (py + 1) * PATCH,
                        j * LANES : (j + 1) * LANES,
                    ]
                    for j in range(PATCH)
                    for k in range(3)
                ],
                axis=0,
            )
            start = (f * down + py) * across
            patches_ref[start : start + across, :] = entries.T[:across].astype(NARROW)

    @pl.loop(0, dim // block, unroll=2)
    def _(n):
        at = pl.ds(pl.multiple_of(n * block, block), block)
        unit_ref[:, at] = dot(patches_ref[...], patch_ref[:, at])

    means = [jnp.zeros((1, dim), WIDE) for _ in range(slots)]
    for b in range(bands):
        rows = slice(b * across, (b + 1) * across)
        embedded = unit_ref[rows, :]
        means[b // down] += jnp.sum(embedded, axis=0, keepdims=True)
        centred = embedded - jnp.mean(embedded, axis=1, keepdims=True)
        scale = lax.rsqrt(jnp.mean(centred * centred, axis=1, keepdims=True) + EPS)
        unit = centred * scale
        unit_ref[rows, :] = unit
        scale_ref[rows, :] = jnp.broadcast_to(scale, (across, LANES))
        normed_ref[rows, :] = (unit * gain_ref[...]).astype(NARROW)
    means = [value * (1.0 / tokens) for value in means]

    qkv_copy.wait()
    proj_copy.wait()
    qkv_ref, proj_ref = qkv_copy_ref, proj_copy_ref

    row_head = lax.broadcasted_iota(jnp.int32, (block, block), 0) // HEAD_DIM
    lane_head = lax.broadcasted_iota(jnp.int32, (block, block), 1) // HEAD_DIM
    average = jnp.where(row_head == lane_head, 1.0 / HEAD_DIM, 0.0).astype(NARROW)

    @pl.loop(0, 2 * dim // block)
    def _(n):
        at = pl.multiple_of(n * block, block)
        both = dot(normed_ref[...], qkv_ref[:, pl.ds(at, block)])
        centred = both - dot(both.astype(NARROW), average)
        scale = lax.rsqrt(dot((centred * centred).astype(NARROW), average) + EPS)
        head_scale_ref[:, pl.ds(at, block)] = scale
        heads_ref[:, pl.ds(at, block)] = (centred * scale).astype(NARROW)

    lane = lax.broadcasted_iota(jnp.int32, (1, LANES), 1)
    sides = [lane < HEAD_DIM, lane >= HEAD_DIM]
    factor = 1.0 / HEAD_DIM**0.5
    pairs = dim // LANES

    def pair_at(index):
        f = index // pairs
        i = index % pairs
        rows = pl.ds(pl.multiple_of(f * tokens, SUB), tokens)
        query_at = pl.ds(pl.multiple_of(i * LANES, LANES), LANES)
        key_at = pl.ds(pl.multiple_of(dim + i * LANES, LANES), LANES)
        return rows, query_at, key_at

    @pl.loop(0, slots * pairs, unroll=8)
    def _(index):
        rows, query_at, key_at = pair_at(index)
        query = heads_ref[rows, query_at]
        key = heads_ref[rows, key_at]
        masks = [jnp.where(side, factor, 0.0).astype(NARROW) for side in sides]
        both = dot_rows(jnp.concatenate([query * mask for mask in masks], axis=0), key)
        for side in range(2):
            exps = jnp.exp(both[side * tokens : (side + 1) * tokens])
            probs = exps * (1.0 / jnp.sum(exps, axis=1, keepdims=True))
            column_ref[pl.ds(2 * index + side, 1), :] = jnp.sum(probs, axis=0, keepdims=True)
            probs_ref[2 * index + side] = probs.astype(NARROW)

    value_weight = qkv_ref.at[:, 2 * dim : 3 * dim]
    head_row = lax.broadcasted_iota(jnp.int32, (HEADS, dim), 0)
    head_lane = lax.broadcasted_iota(jnp.int32, (HEADS, dim), 1) // HEAD_DIM
    own_head = head_row == head_lane
    normed = [normed_ref[f * tokens : (f + 1) * tokens, :] for f in range(slots)]
    weights = [column_ref[f * HEADS : (f + 1) * HEADS, :].astype(NARROW) for f in range(slots)]
    mixed = jnp.concatenate([dot(weights[f], normed[f]) for f in range(slots)], axis=0)
    values = dot(mixed.astype(NARROW), value_weight[...])
    context = jnp.concatenate(
        [
            jnp.broadcast_to(
                jnp.sum(
                    jnp.where(own_head, values[f * HEADS : (f + 1) * HEADS], 0.0),
                    axis=0,
                    keepdims=True,
                )
                * (1.0 / tokens),
                (8, dim),
            )
            for f in range(slots)
        ],
        axis=0,
    )
    mean_rows = jnp.concatenate([jnp.broadcast_to(m, (8, dim)) for m in means], axis=0)
    pooled = mean_rows + dot(context.astype(NARROW), proj_ref[...])
    centred = pooled - jnp.mean(pooled, axis=1, keepdims=True)
    scale = lax.rsqrt(jnp.mean(centred * centred, axis=1, keepdims=True) + EPS)
    unit = centred * scale
    post = unit * post_gain_ref[...]
    text = text_ref[...]
    text = text * lax.rsqrt(jnp.sum(text * text, axis=1, keepdims=True) + EPS)
    along = jnp.sum(post * text, axis=1, keepdims=True)
    length = lax.rsqrt(jnp.sum(post * post, axis=1, keepdims=True) + EPS)
    post_back = (LOSS_SCALE * LOGIT_SCALE) * (length * text - along * length**3 * post)
    unit_back = post_back * post_gain_ref[...]
    pooled_back = scale * (
        unit_back
        - jnp.mean(unit_back, axis=1, keepdims=True)
        - unit * jnp.mean(unit_back * unit, axis=1, keepdims=True)
    )
    token_back = pooled_back * (1.0 / tokens)
    context_back = dot_rows(token_back.astype(NARROW), proj_ref[...])
    by_head = jnp.concatenate(
        [
            jnp.where(own_head, jnp.broadcast_to(context_back[8 * f : 8 * f + 1], (HEADS, dim)), 0.0)
            for f in range(slots)
        ],
        axis=0,
    )
    value_back = dot_rows(by_head.astype(NARROW), value_weight[...]).astype(NARROW)
    for f in range(slots):
        slope_ref[f * HEADS : (f + 1) * HEADS, :] = dot_rows(
            value_back[f * HEADS : (f + 1) * HEADS], normed[f]
        )

    @pl.loop(0, slots * pairs, unroll=16)
    def _(index):
        rows, query_at, key_at = pair_at(index)
        query = heads_ref[rows, query_at]
        key = heads_ref[rows, key_at]
        scores_back = []
        for side in range(2):
            probs = probs_ref[2 * index + side].astype(WIDE)
            slope = slope_ref[pl.ds(2 * index + side, 1), :]
            middle = jnp.sum(probs * slope, axis=1, keepdims=True)
            scores_back.append((probs * (slope - middle)).astype(NARROW))
        query_back = dot(jnp.concatenate(scores_back, axis=0), key)
        key_back = jnp.concatenate(
            [dot(part, query, ((0,), (0,))) for part in scores_back], axis=0
        )
        gradient = jnp.concatenate(
            [
                jnp.where(sides[0], query_back[:tokens], query_back[tokens:]),
                jnp.where(sides[0], key_back[:tokens], key_back[tokens:]),
            ],
            axis=1,
        )
        unit = jnp.concatenate([query, key], axis=1).astype(WIDE)
        plain = dot(gradient.astype(NARROW), average)
        along = dot((gradient * unit).astype(NARROW), average)
        value = factor * (gradient - plain - unit * along)
        back_ref[rows, query_at] = (head_scale_ref[rows, query_at] * value[:, :LANES]).astype(NARROW)
        back_ref[rows, key_at] = (head_scale_ref[rows, key_at] * value[:, LANES:]).astype(NARROW)

    for f in range(slots):
        grad_ref[f * tokens : (f + 1) * tokens, :] = dot(
            weights[f], value_back[f * HEADS : (f + 1) * HEADS], ((0,), (0,))
        )

    @pl.loop(0, dim // block, unroll=2)
    def _(n):
        at = pl.ds(pl.multiple_of(n * block, block), block)
        grad_ref[:, at] += dot_rows(back_ref[...], qkv_ref[at, : 2 * dim])

    tangent_ref[...] = jnp.zeros_like(tangent_ref)
    for b in range(bands):
        rows = slice(b * across, (b + 1) * across)
        f = b // down
        unit = unit_ref[rows, :]
        unit_back = grad_ref[rows, :] * gain_ref[...]
        value = (
            unit_back
            - jnp.mean(unit_back, axis=1, keepdims=True)
            - unit * jnp.mean(unit_back * unit, axis=1, keepdims=True)
        )
        value = scale_ref[rows, :1] * value + token_back[8 * f : 8 * f + 1]
        tangent_ref[b * LANES : b * LANES + across, :] = value.astype(NARROW)

    lines = []
    for f in range(slots):
        entries = dot_rows(
            patch_ref[...], tangent_ref[f * down * LANES : (f + 1) * down * LANES, :]
        ).astype(NARROW)
        for k in range(3):
            for py in range(down):
                lines.append(
                    jnp.concatenate(
                        [
                            entries[
                                (3 * j + k) * PATCH : (3 * j + k + 1) * PATCH,
                                py * LANES : (py + 1) * LANES,
                            ]
                            for j in range(PATCH)
                        ],
                        axis=1,
                    )
                )
    every = dot_rows(jnp.concatenate(lines, axis=0), order_ref[...])
    for f in range(slots):
        frame = every[f * colour_rows : (f + 1) * colour_rows]
        frame = jnp.concatenate(
            [
                jnp.zeros((colour_rows, 2), WIDE),
                frame,
                jnp.zeros((colour_rows, LANES - 2), WIDE),
            ],
            axis=1,
        )
        for t in range(tiles):
            base = t * width
            main = frame[:, base : base + LANES]
            if rem == 0 and width + 4 < LANES:
                main = jnp.where(lane < width + 4, main, 0.0)
            strip_ref[t, f, :colour_rows, :] = main.astype(NARROW)
            if rem > 0:
                tail = [
                    frame[
                        k * height : (k + 1) * height, base + LANES : base + LANES + rem
                    ]
                    for k in range(3)
                ]
                tail.append(jnp.zeros((height, LANES - 3 * rem), WIDE))
                strip_ref[t, f, colour_rows:, :] = jnp.concatenate(tail, axis=1).astype(NARROW)


def tower(
    pixels, patch_weight, norm_gain, qkv_weight, out_weight, post_gain, text_embed, tiles
):
    slots, colours, height, columns = pixels.shape
    dim = norm_gain.shape[0]
    across = columns // PATCH
    down = height // PATCH
    tokens = across * down
    total = slots * tokens
    width = columns // tiles
    rows = colours * height + (height if width + 4 > LANES else 0)
    entries = colours * PATCH * PATCH
    vmem = pl.BlockSpec(memory_space=pltpu.VMEM)
    return pl.pallas_call(
        functools.partial(tower_kernel, tiles),
        out_shape=jax.ShapeDtypeStruct((tiles, slots, rows, LANES), NARROW),
        in_specs=[vmem] * 3 + [pl.BlockSpec(memory_space=pl.ANY)] * 2 + [vmem] * 2,
        out_specs=vmem,
        scratch_shapes=[
            pltpu.VMEM((columns, PATCH * LANES), NARROW),
            pltpu.VMEM((total, entries), NARROW),
            pltpu.VMEM((total, dim), WIDE),
            pltpu.VMEM((total, LANES), WIDE),
            pltpu.VMEM((total, dim), NARROW),
            pltpu.VMEM((total, 2 * dim), NARROW),
            pltpu.VMEM((total, 2 * dim), WIDE),
            pltpu.VMEM((slots * HEADS, tokens, tokens), NARROW),
            pltpu.VMEM((slots * HEADS, tokens), WIDE),
            pltpu.VMEM((slots * HEADS, tokens), WIDE),
            pltpu.VMEM((total, 2 * dim), NARROW),
            pltpu.VMEM((total, dim), WIDE),
            pltpu.VMEM((slots * down * LANES, dim), NARROW),
            pltpu.VMEM(qkv_weight.shape, NARROW),
            pltpu.VMEM(out_weight.shape, NARROW),
            pltpu.VMEM((entries, dim), NARROW),
            pltpu.SemaphoreType.DMA((2,)),
        ],
        compiler_params=pltpu.CompilerParams(vmem_limit_bytes=60 * 1024 * 1024),
        cost_estimate=pl.CostEstimate(
            flops=2 * total * dim * (2 * entries + 4 * dim + 4 * tokens),
            bytes_accessed=2 * (entries * dim + 4 * dim * dim),
            transcendentals=slots * HEADS * tokens * tokens,
        ),
    )(
        pixels.reshape(slots, colours * height, columns),
        patch_weight,
        norm_gain[None],
        qkv_weight,
        out_weight,
        post_gain[None],
        text_embed[None],
    )


def frame_rank(owner):
    frame_ids = jnp.arange(owner.shape[0], dtype=jnp.int32)
    same_owner = owner[:, None] == owner[None, :]
    earlier = frame_ids[None, :] < frame_ids[:, None]
    return jnp.sum((same_owner & earlier).astype(jnp.int32), axis=1)


def local(
    pixels,
    owner,
    patch_weight,
    norm_gain,
    qkv_weight,
    out_weight,
    post_gain,
    text_embed,
    conv_out_weight,
    conv_weight,
    activations,
):
    tile_count = lax.axis_size("tile")
    core_count = lax.axis_size("tm")
    core = lax.axis_index("tm")
    frames, height, width, channels = activations.shape
    slots = pixels.shape[0]
    ranks_all = frame_rank(owner)

    outgoing = tower(
        pixels, patch_weight, norm_gain, qkv_weight, out_weight, post_gain, text_embed, tile_count
    )
    outgoing, origin = lax.optimization_barrier((outgoing, jnp.int32(0)))
    rows = outgoing.shape[2]
    near = lax.all_to_all(outgoing, "tile", split_axis=0, concat_axis=0, tiled=True)
    up = [(i, i + 1) for i in range(tile_count - 1)]
    down = [(j, i) for i, j in up]
    left = lax.ppermute(lax.dynamic_index_in_dim(activations, origin + (width - 1), 2, False), "tile", up)
    right = lax.ppermute(lax.dynamic_index_in_dim(activations, origin, 2, False), "tile", down)

    near = near.reshape(tile_count * slots, rows, LANES)
    pick_all = (owner // core_count) * slots + ranks_all
    code_all = 2 * pick_all + (owner % core_count == core).astype(jnp.int32)
    by_core = lambda values, index: lax.dynamic_slice_in_dim(values, index * frames, frames)
    code = by_core(code_all, core)
    weights = decoder_weights(conv_out_weight, conv_weight, height, width)
    near, code, left, right, *weights = lax.optimization_barrier(
        (near, code, left, right, *weights)
    )
    other = 1 - core
    far = lax.ppermute(jnp.take(near, by_core(pick_all, other), axis=0), "tm", [(0, 1), (1, 0)])
    return decode(
        code,
        near,
        far,
        left,
        right,
        activations,
        weights,
        4,
    )


def solution(mesh):
    placed = (
        P(("groups", "tile", "tm"), None, None, None),
        P("groups"),
        P(),
        P(),
        P(),
        P(),
        P(),
        P("groups"),
        P(),
        P(),
        P(("groups", "tm"), None, "tile", None),
    )
    return jax.shard_map(
        local,
        mesh=mesh,
        in_specs=placed,
        out_specs=P(("groups", "tm"), None, "tile", None),
        check_vma=False,
    )
```
